256 devices in a mesh: layer: 8 (over y, z_lo), row: 32 (over z_hi, x, core).
Axes of the slice: x: 4, y: 4, z: 8 (z_hi: 4, z_lo: 2; z = z_hi * 2 + z_lo), core: 2. Of those that a mesh axis runs over, the one named last changes fastest.
Arguments:
- q_prev: float32 [32, 2048, 2048], P('layer', 'row'), may hold values from -6 to 6
- q_now: float32 [32, 2048, 2048], P('layer', 'row'), may hold values from -6 to 6
- psi_now: float32 [32, 2048, 2048], P('layer', 'row'), may hold values from -6 to 6
- layers_to_modes: float32 [32, 32], replicated, may hold values from -1 to 1
- modes_to_layers: float32 [32, 32], replicated, may hold values from -7 to 7
- stretch: float32 [32], replicated, may hold values from 6.1035156e-05 to 2
Outputs:
- q_next: float32 [32, 2048, 2048], P('layer', 'row')
- psi_next: float32 [32, 2048, 2048], P('layer', 'row')
The draws below stay inside these ranges and needn't reach their ends.
All inputs are finite; a program needn't handle non-finite values.
Results may differ from the reference program's by a relative error of at most 0.003.
Values sent between devices are 32-bit elements; how exact they have to be, the bound alone decides.
No kernel may reach another device: no remote copies, remote signals or barrier semaphores. Data moves between devices by JAX's collectives and lax.ppermute only.
A program may use at most 192 MiB of HBM per device.

```python
import math
import jax
import jax.numpy as jnp
from jax import lax

LAYERS = 32
NY = 2048
NX = 2048


LOWEST_STRETCH = 6.103515625e-05


HIGHEST_STRETCH = 2.0


def stretch_values(key, power):
    spread = jax.random.uniform(key, (LAYERS,), jnp.float32)
    lowest = jnp.min(spread)
    highest = jnp.max(spread)
    position = ((spread - lowest) / (highest - lowest)) ** power
    logs = math.log(LOWEST_STRETCH) + position * (math.log(HIGHEST_STRETCH) - math.log(LOWEST_STRETCH))
    return jnp.clip(jnp.exp(logs), LOWEST_STRETCH, HIGHEST_STRETCH)


def draw_stretch(key, part):
    power = 1.0
    return stretch_values(key, power)


def draw_modes_to_layers(key, part):
    power = 1.0
    shared = stretch_values(key, power)
    key = jax.random.fold_in(key, 7)
    noise = jax.random.truncated_normal(key, -4.0, 4.0, (LAYERS, LAYERS), jnp.float32)
    column_scale = 0.5 * (jnp.sqrt(shared) + shared)
    return noise * column_scale[None, :]


def block_levels(stream_key, dims, shards, low, top_value):
    gain, own = 1.0, jax.random.fold_in(stream_key, 6)
    for dim, parts in shards:
        steps = jnp.exp(jax.random.uniform(jax.random.fold_in(own, dim), (parts,), jnp.float32, low / len(shards), top_value / len(shards)))
        gain = gain * jnp.repeat(steps, dims[dim] // parts).reshape([-1 if axis == dim else 1 for axis in range(len(dims))])
    return gain


def gaussian(own_key, shape, scale, reach, split=(), kind=jnp.bfloat16):
    result = scale * jax.random.normal(own_key, shape, jnp.float32)
    if split:
        result = result * block_levels(own_key, shape, split, -0.22, 0.18)
    return jnp.clip(result, -reach, reach).astype(kind)


def setup_inputs(seed: int = 0) -> dict:
    key_list = jax.random.split(jax.random.key(seed), 7)
    q_prev = gaussian(key_list[0], (LAYERS, NY, NX), 1.0, 6.0, ((0, 8), (1, 32)), jnp.float32)
    q_now = gaussian(key_list[1], (LAYERS, NY, NX), 1.0, 6.0, ((0, 8), (1, 32)), jnp.float32)
    psi_now = gaussian(key_list[2], (LAYERS, NY, NX), 1.0, 6.0, ((0, 8), (1, 32)), jnp.float32)
    layers_to_modes = gaussian(key_list[3], (LAYERS, LAYERS), LAYERS ** -0.5, 1.0, (), jnp.float32)
    modes_to_layers = draw_modes_to_layers(jax.random.fold_in(key_list[6], 71), 0)
    stretch = draw_stretch(jax.random.fold_in(key_list[6], 71), 0)
    return dict(q_prev=q_prev, q_now=q_now, psi_now=psi_now, layers_to_modes=layers_to_modes, modes_to_layers=modes_to_layers, stretch=stretch)


TIME_STEP = 0.1
VISCOSITY = 0.02
HIGHEST = lax.Precision.HIGHEST


def five_point(padded):
    return (padded[..., 2:, 1:-1] + padded[..., :-2, 1:-1] + padded[..., 1:-1, 2:]
            + padded[..., 1:-1, :-2] - 4.0 * padded[..., 1:-1, 1:-1])


def offset(source, row_step, col_step):
    height = source.shape[-2]
    width = source.shape[-1]
    return source[..., 1 + row_step:height - 1 + row_step, 1 + col_step:width - 1 + col_step]


def arakawa(stream, vortex):
    first = ((offset(stream, 0, 1) - offset(stream, 0, -1)) * (offset(vortex, 1, 0) - offset(vortex, -1, 0))
             - (offset(stream, 1, 0) - offset(stream, -1, 0)) * (offset(vortex, 0, 1) - offset(vortex, 0, -1)))
    second = (offset(stream, 0, 1) * (offset(vortex, 1, 1) - offset(vortex, -1, 1))
              - offset(stream, 0, -1) * (offset(vortex, 1, -1) - offset(vortex, -1, -1))
              - offset(stream, 1, 0) * (offset(vortex, 1, 1) - offset(vortex, 1, -1))
              + offset(stream, -1, 0) * (offset(vortex, -1, 1) - offset(vortex, -1, -1)))
    third = (offset(vortex, 1, 0) * (offset(stream, 1, 1) - offset(stream, 1, -1))
             - offset(vortex, -1, 0) * (offset(stream, -1, 1) - offset(stream, -1, -1))
             - offset(vortex, 0, 1) * (offset(stream, 1, 1) - offset(stream, -1, 1))
             + offset(vortex, 0, -1) * (offset(stream, 1, -1) - offset(stream, -1, -1)))
    return (first + second + third) / 12.0


def sine_table(length):
    positions = jnp.arange(length, dtype=jnp.int32) + 1
    product = (positions[:, None] * positions[None, :]) % (2 * (length + 1))
    return jnp.sin(product.astype(jnp.float32) * (math.pi / (length + 1)))


def eigenvalues(length):
    positions = (jnp.arange(length, dtype=jnp.int32) + 1).astype(jnp.float32)
    return 2.0 - 2.0 * jnp.cos(positions * (math.pi / (length + 1)))


def reference(q_prev, q_now, psi_now, layers_to_modes, modes_to_layers, stretch):
    margin_pad = ((0, 0), (1, 1), (1, 1))
    tendency = -arakawa(jnp.pad(psi_now, margin_pad), jnp.pad(q_now, margin_pad))
    inner_lap = five_point(jnp.pad(q_prev, margin_pad))
    tendency = tendency - VISCOSITY * five_point(jnp.pad(inner_lap, margin_pad))
    q_next = q_prev + 2.0 * TIME_STEP * tendency
    rows_table = sine_table(NY)
    cols_table = sine_table(NX)
    row_eigen = eigenvalues(NY)
    col_eigen = eigenvalues(NX)
    scale_back = 4.0 / ((NY + 1) * (NX + 1))

    def solve_mode(inputs):
        weights, stretch_value = inputs
        modal_field = jnp.tensordot(weights, q_next, axes=1, precision=HIGHEST)
        spectrum = jnp.dot(jnp.dot(rows_table, modal_field, precision=HIGHEST, preferred_element_type=jnp.float32),
                           cols_table, precision=HIGHEST, preferred_element_type=jnp.float32)
        solved = -spectrum / (row_eigen[:, None] + col_eigen[None, :] + stretch_value)
        physical = jnp.dot(jnp.dot(rows_table, solved, precision=HIGHEST, preferred_element_type=jnp.float32),
                           cols_table, precision=HIGHEST, preferred_element_type=jnp.float32)
        return physical * scale_back

    psi_modes = lax.map(solve_mode, (layers_to_modes, stretch))
    psi_next = jnp.tensordot(modes_to_layers, psi_modes, axes=1, precision=HIGHEST)
    return q_next, psi_next
```

```python
import functools
import math

import jax
import jax.numpy as jnp
import ml_dtypes
import numpy as np
from jax import lax
from jax.experimental import pallas as pl
from jax.experimental.pallas import tpu as pltpu
from jax.sharding import PartitionSpec as P

TIME_STEP = 0.1
VISCOSITY = 0.02
F32 = jnp.float32
BF16 = jnp.bfloat16
VMEM_LIMIT = 48 * 1024 * 1024
MARGIN = 128


def params():
    return pltpu.CompilerParams(vmem_limit_bytes=VMEM_LIMIT)


def half_table(length):
    positions = np.arange(1, length // 2 + 1, dtype=np.int64)
    product = (2 * positions[:, None] * positions[None, :]) % (2 * (length + 1))
    table = np.sin(product.astype(np.float64) * (math.pi / (length + 1)))
    high = table.astype(np.float32).astype(ml_dtypes.bfloat16)
    low = (table - high.astype(np.float64)).astype(np.float32).astype(ml_dtypes.bfloat16)
    return high, low


def column_eigen(length, shards):
    positions = np.arange(1, length // 2 + 1, dtype=np.float64)
    waves = np.stack([length + 1 - 2 * positions, 2 * positions])
    eigen = 4.0 * np.sin(waves * (math.pi / (2 * (length + 1)))) ** 2
    return eigen.astype(np.float32).reshape(2, shards, -1)


def split(value):
    high = value.astype(BF16)
    low = (value - high.astype(F32)).astype(BF16)
    return high, low


def dot(left, right):
    return jnp.dot(left, right, preferred_element_type=F32)


def flip_lanes(value):
    width = value.shape[1]
    order = 127 - lax.broadcasted_iota(jnp.int32, (value.shape[0], 128), 1)
    blocks = [
        jnp.take_along_axis(value[:, start : start + 128], order, axis=1)
        for start in range(width - 128, -1, -128)
    ]
    return jnp.concatenate(blocks, axis=1)


def alternating(width):
    lane = lax.broadcasted_iota(jnp.int32, (1, width), 1)
    return jnp.where(lane % 2 == 0, 1.0, -1.0).astype(F32)


def stencil_kernel(edge, prev, now, psi, top, bottom, q_out, fold, p_ext, z_ext, q_ext, l_ext):
    rows, cols = prev.shape[1], prev.shape[2]
    wide = cols + MARGIN

    def east(value):
        return pltpu.roll(value, wide - 1, 1)

    def west(value):
        return pltpu.roll(value, 1, 1)

    @pl.when(pl.program_id(0) == 0)
    def _():
        for ext in (p_ext, z_ext, q_ext, l_ext):
            ext[:, cols:] = jnp.zeros((rows + 16, MARGIN), F32)

    p_ext[8 : 8 + rows, :cols] = psi[0]
    z_ext[8 : 8 + rows, :cols] = now[0]
    q_ext[8 : 8 + rows, :cols] = prev[0]
    p_ext[7:8, :cols] = top[0, 0:1]
    z_ext[7:8, :cols] = top[0, 1:2]
    q_ext[6:8, :cols] = top[0, 2:4]
    p_ext[8 + rows : 9 + rows, :cols] = bottom[0, 0:1]
    z_ext[8 + rows : 9 + rows, :cols] = bottom[0, 1:2]
    q_ext[8 + rows : 10 + rows, :cols] = bottom[0, 2:4]

    def window(ext, tile):
        value = ext[pl.ds(pl.multiple_of(8 * tile, 8), 24), :]
        return value[7:15], value[8:16], value[9:17]

    def ghost(row):
        here = q_ext[row : row + 1, :]
        value = q_ext[row - 1 : row, :] + q_ext[row + 1 : row + 2, :] + east(here) + west(here) - 4.0 * here
        return value[:, :cols]

    l_ext[7:8, :cols] = ghost(7) * edge[0]
    l_ext[8 + rows : 9 + rows, :cols] = ghost(8 + rows) * edge[1]

    def inner(tile, carry):
        north, here, south = window(q_ext, tile)
        value = north + south + east(here) + west(here) - 4.0 * here
        l_ext[pl.ds(pl.multiple_of(8 * tile + 8, 8), 8), :cols] = value[:, :cols]
        return carry

    lax.fori_loop(0, rows // 8, inner, 0)

    def outer(tile, carry):
        zn, zc, zs = window(z_ext, tile)
        pn, pc, ps = window(p_ext, tile)
        zne, zce, zse = east(zn), east(zc), east(zs)
        znw, zcw, zsw = west(zn), west(zc), west(zs)
        down = zs - zn
        from_east = pc * ((zsw - znw) + down) + ps * (zsw - zc) + pn * (zc - znw)
        from_west = ps * (zc - zse) + pn * (zne - zc) - pc * ((zse - zne) + down)
        across = zce - zcw
        jacobian = pn * (across + (zne - znw)) - ps * (across + (zse - zsw))
        jacobian = jacobian + east(from_east) + west(from_west)
        ln, lc, ls = window(l_ext, tile)
        friction = ln + ls + east(lc) + west(lc) - 4.0 * lc
        here = q_ext[pl.ds(pl.multiple_of(8 * tile + 8, 8), 8), :]
        value = here - (2.0 * TIME_STEP / 12.0) * jacobian - (2.0 * TIME_STEP * VISCOSITY) * friction
        value = value[:, :cols]
        at = pl.ds(pl.multiple_of(8 * tile, 8), 8)
        q_out[0, at, :] = value
        lower, upper = value[:, : cols // 2], flip_lanes(value[:, cols // 2 :])
        fold[0, 0, at, :] = (lower + upper) * alternating(cols // 2)
        fold[1, 0, at, :] = lower - upper
        return carry

    lax.fori_loop(0, rows // 8, outer, 0)


def stencil(edge, q_prev, q_now, psi_now, top, bottom):
    layers, rows, cols = q_prev.shape
    block = pl.BlockSpec((1, rows, cols), lambda i: (i, 0, 0))
    rim = pl.BlockSpec((1, 4, cols), lambda i: (i, 0, 0))
    ext = pltpu.VMEM((rows + 16, cols + MARGIN), F32)
    return pl.pallas_call(
        stencil_kernel,
        grid=(layers,),
        in_specs=[pl.BlockSpec(memory_space=pltpu.SMEM), block, block, block, rim, rim],
        out_specs=[block, pl.BlockSpec((2, 1, rows, cols // 2), lambda i: (0, i, 0, 0))],
        out_shape=[
            jax.ShapeDtypeStruct(q_prev.shape, F32),
            jax.ShapeDtypeStruct((2, layers, rows, cols // 2), F32),
        ],
        scratch_shapes=[ext, ext, ext, ext],
        compiler_params=params(),
        name="stencil",
    )(edge, q_prev, q_now, psi_now, top, bottom)


def forward_kernel(source, table_high, table_low, result, high, low):
    @pl.when(pl.program_id(0) == 0)
    def _():
        high[...], low[...] = split(source[0])

    value = dot(high[...], table_high[...]) + dot(low[...], table_high[...]) + dot(high[...], table_low[...])
    width = result.shape[2]
    for part in range(result.shape[0]):
        result[part] = value[:, part * width : (part + 1) * width]


def forward(fold, parity, table_high, table_low, shards):
    depth = table_high.shape[0]
    lines = fold.shape[1] * fold.shape[2]
    width = depth // shards
    step = 2 * width
    column = pl.BlockSpec((depth, step), lambda i: (0, i))
    return pl.pallas_call(
        forward_kernel,
        grid=(depth // step,),
        in_specs=[pl.BlockSpec((1, lines, depth), lambda i: (parity, 0, 0)), column, column],
        out_specs=pl.BlockSpec((2, lines, width), lambda i: (i, 0, 0)),
        out_shape=jax.ShapeDtypeStruct((shards, lines, width), F32),
        scratch_shapes=[pltpu.VMEM((lines, depth), BF16)] * 2,
        compiler_params=params(),
        cost_estimate=pl.CostEstimate(flops=6 * lines * depth * depth, bytes_accessed=6 << 20, transcendentals=0),
        name="forward",
    )(fold.reshape(2, lines, depth), table_high, table_low)


def project_kernel(source, mix_high, mix_low, ratio, modal, ends, power):
    layers, rows, width = source.shape

    @pl.when(pl.program_id(0) == 0)
    def _():
        ends[...] = jnp.zeros(ends.shape, F32)
        power[...] = jnp.ones(power.shape, F32)

    tiles = [source[:, 8 * t : 8 * t + 8, :].reshape(8 * layers, width) for t in range(rows // 8)]
    high, low = split(jnp.concatenate(tiles, axis=1))
    mixed = dot(mix_high[...], high) + dot(mix_low[...], high) + dot(mix_high[...], low)
    decay = ratio[...]
    last, first, scale = ends[0], ends[1], power[...]
    for t in range(rows // 8):
        block = mixed[:, t * width : (t + 1) * width].reshape(8, layers, width)
        modal[8 * t : 8 * t + 8] = block
        for row in range(8):
            last = decay * last + block[row]
            first = first + scale * block[row]
            scale = scale * decay
    ends[0] = last
    ends[1] = first
    power[...] = scale


def project(stacked, mix_high, mix_low, ratio):
    layers, rows, width = stacked.shape
    step = 16
    whole = pl.BlockSpec(mix_high.shape, lambda i: (0, 0))
    return pl.pallas_call(
        project_kernel,
        grid=(rows // step,),
        in_specs=[
            pl.BlockSpec((layers, step, width), lambda i: (0, i, 0)),
            whole,
            whole,
            pl.BlockSpec((layers, width), lambda i: (0, 0)),
        ],
        out_specs=[
            pl.BlockSpec((step, layers, width), lambda i: (i, 0, 0)),
            pl.BlockSpec((2, layers, width), lambda i: (0, 0, 0)),
        ],
        out_shape=[
            jax.ShapeDtypeStruct((rows, layers, width), F32),
            jax.ShapeDtypeStruct((2, layers, width), F32),
        ],
        scratch_shapes=[pltpu.VMEM((layers, width), F32)],
        compiler_params=params(),
        name="project",
    )(stacked, mix_high, mix_low, ratio)


def solve_kernel(modal, carry, ratio, scale, mix_high, mix_low, result, down, up):
    rows, layers, width = modal.shape
    step = result.shape[1]
    decay = ratio[...]

    @pl.when(pl.program_id(0) == 0)
    def _():
        def forth(row, value):
            value = decay * value + modal[row]
            down[row] = value
            return value

        lax.fori_loop(0, rows, forth, carry[0], unroll=8)
        up[...] = carry[1]

    base = rows - step * (pl.program_id(0) + 1)
    beyond, factor = up[...], scale[...]
    solved = [None] * step
    for row in range(step - 1, -1, -1):
        value = decay * beyond
        beyond = modal[base + row] + value
        solved[row] = factor * (down[base + row] + value)
    up[...] = beyond
    tiles = [
        jnp.stack(solved[8 * t : 8 * t + 8]).reshape(8 * layers, width) for t in range(step // 8)
    ]
    high, low = split(jnp.concatenate(tiles, axis=1))
    mixed = dot(mix_high[...], high) + dot(mix_low[...], high) + dot(mix_high[...], low)
    for t in range(step // 8):
        result[:, 8 * t : 8 * t + 8, :] = mixed[:, t * width : (t + 1) * width].reshape(layers, 8, width)


def solve(modal, carry, ratio, scale, mix_high, mix_low):
    rows, layers, width = modal.shape
    step = 16
    whole = pl.BlockSpec(mix_high.shape, lambda i: (0, 0))
    field = pl.BlockSpec((layers, width), lambda i: (0, 0))
    return pl.pallas_call(
        solve_kernel,
        grid=(rows // step,),
        in_specs=[
            pl.BlockSpec((rows, layers, width), lambda i: (0, 0, 0)),
            pl.BlockSpec((2, layers, width), lambda i: (0, 0, 0)),
            field,
            field,
            whole,
            whole,
        ],
        out_specs=pl.BlockSpec((layers, step, width), lambda i: (0, rows // step - 1 - i, 0)),
        out_shape=jax.ShapeDtypeStruct((layers, rows, width), F32),
        scratch_shapes=[pltpu.VMEM((rows, layers, width), F32), pltpu.VMEM((layers, width), F32)],
        compiler_params=params(),
        name="solve",
    )(modal, carry, ratio, scale, mix_high, mix_low)


def gather_split(source, high, low):
    width = source.shape[2]
    for part in range(source.shape[0]):
        high[:, part * width : (part + 1) * width], low[:, part * width : (part + 1) * width] = split(source[part])


def inverse_odd_kernel(source, table_high, table_low, result, high, low):
    @pl.when(pl.program_id(0) == 0)
    def _():
        gather_split(source, high, low)

    value = dot(high[...], table_high[...]) + dot(low[...], table_high[...]) + dot(high[...], table_low[...])
    result[...] = value * alternating(value.shape[1])


def inverse_odd(source, table_high, table_low):
    shards, lines, width = source.shape
    depth = shards * width
    step = 256
    column = pl.BlockSpec((depth, step), lambda i: (0, i))
    return pl.pallas_call(
        inverse_odd_kernel,
        grid=(depth // step,),
        in_specs=[pl.BlockSpec(source.shape, lambda i: (0, 0, 0)), column, column],
        out_specs=pl.BlockSpec((lines, step), lambda i: (0, i)),
        out_shape=jax.ShapeDtypeStruct((lines, depth), F32),
        scratch_shapes=[pltpu.VMEM((lines, depth), BF16)] * 2,
        compiler_params=params(),
        name="inverse_odd",
    )(source, table_high, table_low)


def inverse_even_kernel(source, odd, table_high, table_low, result, high, low):
    @pl.when(pl.program_id(0) == 0)
    def _():
        gather_split(source, high, low)

    value = dot(high[...], table_high[...]) + dot(low[...], table_high[...]) + dot(high[...], table_low[...])
    step = value.shape[1]
    count = result.shape[1] // step
    index = pl.program_id(0)
    result[:, pl.ds(pl.multiple_of(index * step, step), step)] = odd[...] + value
    result[:, pl.ds(pl.multiple_of((count - 1 - index) * step, step), step)] = flip_lanes(odd[...] - value)


def inverse_even(source, odd, table_high, table_low):
    shards, lines, width = source.shape
    depth = shards * width
    step = 256
    column = pl.BlockSpec((depth, step), lambda i: (0, i))
    return pl.pallas_call(
        inverse_even_kernel,
        grid=(depth // step,),
        in_specs=[
            pl.BlockSpec(source.shape, lambda i: (0, 0, 0)),
            pl.BlockSpec((lines, step), lambda i: (0, i)),
            column,
            column,
        ],
        out_specs=pl.BlockSpec((lines, 2 * depth), lambda i: (0, 0)),
        out_shape=jax.ShapeDtypeStruct((lines, 2 * depth), F32),
        scratch_shapes=[pltpu.VMEM((lines, depth), BF16)] * 2,
        compiler_params=params(),
        name="inverse_even",
    )(source, odd, table_high, table_low)


def interface(ends, theta, rows):
    blocks = lax.axis_size("row")
    me = lax.axis_index("row")
    unit = rows * theta

    def decay(count):
        return jnp.exp(-unit * count.astype(F32))

    from_above = jnp.zeros_like(theta)
    from_below = jnp.zeros_like(theta)
    group = 1
    total = ends
    for radix in (2, 4, 4):
        place = (me // group) % radix
        inside = me % group
        parts = [total]
        for shift in range(1, radix):
            pairs = []
            for target in range(blocks):
                spot = (target // group) % radix
                pairs.append((target + ((spot + shift) % radix - spot) * group, target))
            parts.append(lax.ppermute(total, "row", pairs))
        last = jnp.zeros_like(theta)
        first = jnp.zeros_like(theta)
        for shift, part in enumerate(parts):
            spot = (place + shift) % radix
            last = last + decay(group * (radix - 1 - spot)) * part[0]
            first = first + decay(group * spot) * part[1]
            if shift:
                above = jnp.where(spot < place, decay(jnp.maximum(group * (place - 1 - spot), 0) + inside), 0.0)
                below = jnp.where(spot > place, decay(jnp.maximum(group * (spot - place - 1), 0) + group - 1 - inside), 0.0)
                from_above = from_above + above * part[0]
                from_below = from_below + below * part[1]
        total = jnp.stack([last, first])
        group *= radix
    span = jnp.exp(-theta * (rows * blocks + 1))
    wall = jnp.exp(-theta) / (1.0 - span * span)
    from_above = from_above + decay(me) * wall * (span * total[0] - total[1])
    from_below = from_below + decay(blocks - 1 - me) * wall * (span * total[1] - total[0])
    return jnp.stack([from_above, from_below])


def block_mix(weights, to_modes):
    count = weights.shape[0]
    eye = jnp.eye(8, dtype=F32)
    if to_modes:
        big = eye[:, None, None, :] * weights[None, :, :, None]
    else:
        big = weights[:, None, None, :] * eye[None, :, :, None]
    big = big.reshape(8 * count, 8 * count)
    high = lax.reduce_precision(big, 8, 7)
    return high.astype(BF16), (big - high).astype(BF16)


def on_device(q_prev, q_now, psi_now, layers_to_modes, modes_to_layers, stretch):
    layer_count, row_count, col_count = q_prev.shape
    blocks = lax.axis_size("row")
    shards = lax.axis_size("layer")
    me = lax.axis_index("row")
    table_high, table_low = (jnp.asarray(value) for value in half_table(col_count))

    last = jnp.concatenate([psi_now[:, -1:], q_now[:, -1:], q_prev[:, -2:]], axis=1)
    initial = jnp.concatenate([psi_now[:, :1], q_now[:, :1], q_prev[:, :2]], axis=1)
    up = [(i, i + 1) for i in range(blocks - 1)]
    down = [(j, i) for i, j in up]
    top = lax.ppermute(last, "row", up)
    bottom = lax.ppermute(initial, "row", down)
    edge = jnp.stack([me > 0, me < blocks - 1]).astype(F32)
    q_next, fold = stencil(edge, q_prev, q_now, psi_now, top, bottom)

    to_modes = block_mix(layers_to_modes, True)
    to_layers = block_mix(modes_to_layers, False)
    eigen = jnp.asarray(column_eigen(col_count, shards))
    eigen = lax.dynamic_index_in_dim(eigen, lax.axis_index("layer"), 1, keepdims=False)
    shift = eigen[:, None, :] + stretch[None, :, None]
    theta = 2.0 * jnp.arcsinh(0.5 * jnp.sqrt(shift))
    ratio = jnp.exp(-theta)
    scale = (-2.0 / (col_count + 1)) / jnp.sqrt(shift * (4.0 + shift))

    returned = []
    for chunk in range(2):
        spectrum = forward(fold, chunk, table_high, table_low, shards)
        stacked = lax.all_to_all(spectrum, "layer", split_axis=0, concat_axis=0, tiled=True)
        stacked = stacked.reshape(shards * layer_count, row_count, -1)
        modal, ends = project(stacked, *to_modes, ratio[chunk])
        carry = interface(ends, theta[chunk], row_count)
        layered = solve(modal, carry, ratio[chunk], scale[chunk], *to_layers)
        layered = layered.reshape(shards, layer_count * row_count, -1)
        returned.append(lax.all_to_all(layered, "layer", split_axis=0, concat_axis=0, tiled=True))
    odd = inverse_odd(returned[0], table_high, table_low)
    psi_next = inverse_even(returned[1], odd, table_high, table_low)
    return (q_next, psi_next.reshape(q_prev.shape))


def solution(mesh):
    return jax.shard_map(
        on_device,
        mesh=mesh,
        in_specs=(
            P("layer", "row", None),
            P("layer", "row", None),
            P("layer", "row", None),
            P(),
            P(),
            P(),
        ),
        out_specs=(P("layer", "row", None), P("layer", "row", None)),
        check_vma=False,
    )
```

```python
import functools
import math

import jax
import jax.numpy as jnp
import ml_dtypes
import numpy as np
from jax import lax
from jax.experimental import pallas as pl
from jax.experimental.pallas import tpu as pltpu
from jax.sharding import PartitionSpec as P

TIME_STEP = 0.1
VISCOSITY = 0.02
F32 = jnp.float32
BF16 = jnp.bfloat16
LANES = 128
LAG = 2


def params(megabytes):
    return pltpu.CompilerParams(vmem_limit_bytes=megabytes << 20)


def half_table(length):
    positions = np.arange(1, length // 2 + 1, dtype=np.int64)
    product = (2 * positions[:, None] * positions[None, :]) % (2 * (length + 1))
    table = np.sin(product.astype(np.float64) * (math.pi / (length + 1)))
    high = table.astype(np.float32).astype(ml_dtypes.bfloat16)
    low = (table - high.astype(np.float64)).astype(np.float32).astype(ml_dtypes.bfloat16)
    return high, low


def column_eigen(length, shards):
    positions = np.arange(1, length // 2 + 1, dtype=np.float64)
    waves = np.stack([length + 1 - 2 * positions, 2 * positions])
    eigen = 4.0 * np.sin(waves * (math.pi / (2 * (length + 1)))) ** 2
    eigen = eigen.astype(np.float32).reshape(2, shards, -1)
    return np.concatenate([eigen[0], eigen[1]], axis=1)


def split(value):
    high = value.astype(BF16)
    low = (value - high.astype(F32)).astype(BF16)
    return high, low


def dot(left, right):
    return jnp.dot(left, right, preferred_element_type=F32)


def three_dots(high, low, table_high, table_low):
    return dot(high, table_high) + dot(low, table_high) + dot(high, table_low)


def alternating(shape):
    lane = lax.broadcasted_iota(jnp.int32, shape, 1)
    return jnp.where(lane % 2 == 0, 1.0, -1.0).astype(F32)


def rim_kernel(prev_first, now_first, psi_first, prev_last, now_last, psi_last, initial, last):
    rows = prev_last.shape[1]
    initial[:, 0:1] = psi_first[:, 0:1]
    initial[:, 1:2] = now_first[:, 0:1]
    initial[:, 2:4] = prev_first[:, 0:2]
    last[:, 0:1] = psi_last[:, rows - 1 :]
    last[:, 1:2] = now_last[:, rows - 1 :]
    last[:, 2:4] = prev_last[:, rows - 2 :]


def rims(q_prev, q_now, psi_now):
    layers, rows, cols = q_prev.shape
    first = pl.BlockSpec((layers, 8, cols), lambda i: (0, 0, 0))
    final = pl.BlockSpec((layers, 8, cols), lambda i: (0, rows // 8 - 1, 0))
    rim = jax.ShapeDtypeStruct((layers, 4, cols), F32)
    whole = pl.BlockSpec(rim.shape, lambda i: (0, 0, 0))
    return pl.pallas_call(
        rim_kernel,
        grid=(1,),
        in_specs=[first, first, first, final, final, final],
        out_specs=[whole, whole],
        out_shape=[rim, rim],
        compiler_params=params(62),
        name="rims",
    )(q_prev, q_now, psi_now, q_prev, q_now, psi_now)


def fill(ext, start, source, index, first, rows):
    for c in range(ext.shape[0]):
        ext[c, start : start + rows, :] = source[(*index, slice(first, first + rows), slice(LANES * c, LANES * (c + 1)))]


def shift_columns(source, to_east, to_west):
    count, rows, width = source.shape
    lane = lax.broadcasted_iota(jnp.int32, (rows, width), 1)
    east, west = {count: 0.0}, {-1: 0.0}

    def store(c):
        to_east[c] = jnp.where(lane == width - 1, east[c + 1], east[c])
        to_west[c] = jnp.where(lane == 0, west[c - 1], west[c])

    for c in range(count + LAG):
        if c < count:
            value = source[c]
            east[c] = pltpu.roll(value, width - 1, 1)
            west[c] = pltpu.roll(value, 1, 1)
        if c >= LAG:
            store(c - LAG)


def advance(fields, q_held, high, low, layer, wall):
    p, z, ze, zw, q, qe, qw = fields
    count, _, width = p.shape
    rows = q_held.shape[1]
    lane = lax.broadcasted_iota(jnp.int32, (rows, width), 1)
    third = -2.0 * TIME_STEP / 12.0
    drag = -2.0 * TIME_STEP * VISCOSITY
    middle, east, west = {}, {count: 0.0}, {-1: 0.0}

    def tendency(c):
        def here(ext, row=0):
            return ext[c, 8 + row : 8 + row + rows, :]

        pn, pc, ps = here(p, -1), here(p), here(p, 1)
        zn, zc, zs = here(z, -1), here(z), here(z, 1)
        zne, zce, zse = here(ze, -1), here(ze), here(ze, 1)
        znw, zcw, zsw = here(zw, -1), here(zw), here(zw, 1)
        qc = here(q)
        near = here(q, -1) + here(q, 1)
        far = here(q, -2) + here(q, 2)
        down = zs - zn
        beside = 2.0 * near - 8.0 * qc
        from_east = pc * ((zsw - znw) + down) + ps * (zsw - zc) + pn * (zc - znw)
        from_west = ps * (zc - zse) + pn * (zne - zc) - pc * ((zse - zne) + down)
        from_east = third * from_east + drag * (beside + here(qe))
        from_west = third * from_west + drag * (beside + here(qw))
        east[c] = pltpu.roll(from_east, width - 1, 1)
        west[c] = pltpu.roll(from_west, 1, 1)
        across = zce - zcw
        own = pn * (across + (zne - znw)) - ps * (across + (zse - zsw))
        bulk = far - 8.0 * near + 20.0 * qc - wall * qc
        if c == 0:
            bulk = bulk - jnp.where(lane == 0, qc, 0.0)
        if c == count - 1:
            bulk = bulk - jnp.where(lane == width - 1, qc, 0.0)
        middle[c] = qc + third * own + drag * bulk

    def finish(c):
        value = middle[c] + jnp.where(lane == width - 1, east[c + 1], east[c])
        value = value + jnp.where(lane == 0, west[c - 1], west[c])
        q_held[layer, :, width * c : width * (c + 1)] = value

    for c in range(count + LAG):
        if c < count:
            tendency(c)
        if c >= LAG:
            finish(c - LAG)

    order = width - 1 - lane
    sign = alternating((rows, width))
    pairs = {}

    def load(c):
        upper = q_held[layer, :, width * (count - 1 - c) : width * (count - c)]
        pairs[c] = q_held[layer, :, width * c : width * (c + 1)], jnp.take_along_axis(upper, order, axis=1)

    def store(c):
        lower, upper = pairs[c]
        column = slice(width * c, width * (c + 1))
        for parity, value in enumerate(((lower + upper) * sign, lower - upper)):
            line = pl.ds(pl.multiple_of((parity * q_held.shape[0] + layer) * rows, rows), rows)
            high[line, column], low[line, column] = split(value)

    for c in range(count // 2 + LAG):
        if c < count // 2:
            load(c)
        if c >= LAG:
            store(c - LAG)


def step_kernel(blocks, place, prev, now, psi, top, bottom, table_high, table_low, q_out, spectrum, *scratch):
    fields, q_held, p, z, ze, zw, q, qe, qw, high, low, held, sems, q_sems, sems_out = scratch
    layers, rows, _ = prev.shape
    shards, lines, width = held.shape
    width //= 2
    count = table_high.shape[1] // width
    index = pl.program_id(0)

    def load(layer, which):
        source = (psi, now, prev)[which]
        return pltpu.make_async_copy(source.at[layer], fields.at[layer, which], sems.at[layer, which])

    def save(layer):
        return pltpu.make_async_copy(q_held.at[layer], q_out.at[layer], q_sems.at[layer])

    def send(step):
        block = pl.ds(step * count, count)
        return pltpu.make_async_copy(held.at[block], spectrum.at[block], sems_out.at[step])

    @pl.when(index == 0)
    def _():
        for layer in range(2):
            for which in range(3):
                load(layer, which).start()

    @pl.when(index < layers)
    def _():
        for which in range(3):
            load(index, which).wait()

        @pl.when(index + 2 < layers)
        def _():
            for which in range(3):
                load(index + 2, which).start()

        for which, ext in enumerate((p, z, q)):
            fill(ext, 8, fields, (index, which), 0, rows)
            first, size = ((0, 1), (1, 1), (2, 2))[which]
            fill(ext, 8 - size, top, (index,), first, size)
            fill(ext, 8 + rows, bottom, (index,), first, size)
        shift_columns(z, ze, zw)
        shift_columns(q, qe, qw)
        row = lax.broadcasted_iota(jnp.int32, (rows, LANES), 0)
        wall_above = jnp.where(place[0] == 0, 0, -1)
        wall_below = jnp.where(place[0] == blocks - 1, rows - 1, -1)
        wall = jnp.where((row == wall_above) | (row == wall_below), 1.0, 0.0).astype(F32)
        advance((p, z, ze, zw, q, qe, qw), q_held, high, low, index, wall)
        save(index).start()

    @pl.when(index >= layers)
    def _():
        step = index - layers
        value = three_dots(high[...], low[...], table_high[...], table_low[...])
        for part in range(count):
            column = slice(part * width, (part + 1) * width)
            held[step * count + part, :, :width] = value[:lines, column]
            held[step * count + part, :, width:] = value[lines:, column]
        send(step).start()

    @pl.when(index == pl.num_programs(0) - 1)
    def _():
        for layer in range(layers):
            save(layer).wait()
        for step in range(shards // count):
            send(step).wait()


def step_forward(place, q_prev, q_now, psi_now, top, bottom, table_high, table_low, shards, blocks):
    layers, rows, cols = q_prev.shape
    depth = cols // 2
    lines = layers * rows
    width = depth // shards
    step = 2 * width
    steps = depth // step
    hbm = pl.BlockSpec(memory_space=pltpu.HBM)
    rim = pl.BlockSpec((layers, 4, cols), lambda i: (0, 0, 0))
    column = pl.BlockSpec((depth, step), lambda i: (0, jnp.maximum(i - layers, 0)))
    return pl.pallas_call(
        functools.partial(step_kernel, blocks),
        grid=(layers + steps,),
        in_specs=[pl.BlockSpec(memory_space=pltpu.SMEM), hbm, hbm, hbm, rim, rim, column, column],
        out_specs=[hbm, hbm],
        out_shape=[
            jax.ShapeDtypeStruct(q_prev.shape, F32),
            jax.ShapeDtypeStruct((shards, lines, 2 * width), F32),
        ],
        scratch_shapes=[
            pltpu.VMEM((layers, 3, rows, cols), F32),
            pltpu.VMEM((layers, rows, cols), F32),
        ]
        + [pltpu.VMEM((cols // LANES, rows + 16, LANES), F32)] * 7
        + [pltpu.VMEM((2 * lines, depth), BF16)] * 2
        + [
            pltpu.VMEM((shards, lines, 2 * width), F32),
            pltpu.SemaphoreType.DMA((layers, 3)),
            pltpu.SemaphoreType.DMA((layers,)),
            pltpu.SemaphoreType.DMA((steps,)),
        ],
        compiler_params=params(62),
        cost_estimate=pl.CostEstimate(flops=12 * lines * depth * depth, bytes_accessed=16 << 20, transcendentals=0),
        name="step_forward",
    )(place, q_prev, q_now, psi_now, top, bottom, table_high, table_low)


def prepare_kernel(shard, eigen, stretch, to_modes, to_layers, theta, ratio, scale, in_high, in_low, out_high, out_low):
    modes, width = theta.shape
    wave = eigen[pl.ds(shard[0], 1), :]
    for mode in range(modes):
        theta[mode : mode + 1, :] = wave + stretch[mode]
    shift = theta[...]
    half = 0.5 * jnp.sqrt(shift)
    angle = 2.0 * jnp.log1p(half + half * half / (1.0 + jnp.sqrt(1.0 + half * half)))
    theta[...] = angle
    ratio[...] = jnp.exp(-angle)
    scale[...] = (-2.0 / (width * eigen.shape[0] + 1)) / jnp.sqrt(shift * (4.0 + shift))

    size = 8 * modes
    line = lax.broadcasted_iota(jnp.int32, (size, modes), 0)
    index = lax.broadcasted_iota(jnp.int32, (size, modes), 1)
    by_layer = (line // 8 == index).astype(F32)
    by_mode = (line % modes == index).astype(F32)
    down = lax.broadcasted_iota(jnp.int32, (size, size), 0)
    along = lax.broadcasted_iota(jnp.int32, (size, size), 1)

    def exact(left, right, sides):
        return lax.dot_general(
            left, right, ((sides, ((), ()))), precision=lax.Precision.HIGHEST, preferred_element_type=F32
        )

    spread = exact(exact(by_mode, to_modes[...], ((1,), (0,))), by_layer, ((1,), (1,)))
    in_high[...], in_low[...] = split(jnp.where(down // modes == along % 8, spread, 0.0))
    spread = exact(exact(by_layer, to_layers[...], ((1,), (0,))), by_mode, ((1,), (1,)))
    out_high[...], out_low[...] = split(jnp.where(down % 8 == along // modes, spread, 0.0))


def prepare(shard, eigen, stretch, to_modes, to_layers):
    modes, width = stretch.shape[0], eigen.shape[1]
    field = jax.ShapeDtypeStruct((modes, width), F32)
    mix = jax.ShapeDtypeStruct((8 * modes, 8 * modes), BF16)
    vmem, smem = pl.BlockSpec(memory_space=pltpu.VMEM), pl.BlockSpec(memory_space=pltpu.SMEM)
    return pl.pallas_call(
        prepare_kernel,
        in_specs=[smem, vmem, smem, vmem, vmem],
        out_specs=[vmem] * 7,
        out_shape=[field, field, field, mix, mix, mix, mix],
        compiler_params=params(8),
        name="prepare",
    )(shard, eigen, stretch, to_modes, to_layers)


def project_kernel(source, mix_high, mix_low, ratio, modal, ends, power):
    layers, rows, width = source.shape

    @pl.when(pl.program_id(0) == 0)
    def _():
        ends[...] = jnp.zeros(ends.shape, F32)
        power[...] = jnp.ones(power.shape, F32)

    decay = ratio[...]
    last, first, scale = ends[0], ends[1], power[...]
    for t in range(rows // 8):
        high, low = split(source[:, 8 * t : 8 * t + 8, :].reshape(8 * layers, width))
        mixed = dot(mix_high[...], high) + dot(mix_low[...], high) + dot(mix_high[...], low)
        block = mixed.reshape(8, layers, width)
        modal[8 * t : 8 * t + 8] = block
        for row in range(8):
            last = decay * last + block[row]
            first = first + scale * block[row]
            scale = scale * decay
    ends[0] = last
    ends[1] = first
    power[...] = scale


def project(stacked, mix_high, mix_low, ratio):
    layers, rows, width = stacked.shape
    step = 16
    whole = pl.BlockSpec(mix_high.shape, lambda i: (0, 0))
    return pl.pallas_call(
        project_kernel,
        grid=(rows // step,),
        in_specs=[
            pl.BlockSpec((layers, step, width), lambda i: (0, i, 0)),
            whole,
            whole,
            pl.BlockSpec((layers, width), lambda i: (0, 0)),
        ],
        out_specs=[
            pl.BlockSpec((step, layers, width), lambda i: (i, 0, 0)),
            pl.BlockSpec((2, layers, width), lambda i: (0, 0, 0)),
        ],
        out_shape=[
            jax.ShapeDtypeStruct((rows, layers, width), F32),
            jax.ShapeDtypeStruct((2, layers, width), F32),
        ],
        scratch_shapes=[pltpu.VMEM((layers, width), F32)],
        compiler_params=params(12),
        name="project",
    )(stacked, mix_high, mix_low, ratio)


RADICES = (2, 4, 4)


def exchange(total, level, blocks):
    radix, group = RADICES[level], math.prod(RADICES[:level])
    parts = []
    for shift in range(1, radix):
        pairs = []
        for target in range(blocks):
            spot = (target // group) % radix
            pairs.append((target + ((spot + shift) % radix - spot) * group, target))
        parts.append(lax.ppermute(total, "row", pairs))
    return parts


def decayed(unit, count):
    return jnp.exp(-unit * count.astype(F32))


def join(unit, me, parts, level):
    radix, group = RADICES[level], math.prod(RADICES[:level])
    place = (me // group) % radix
    last = jnp.zeros_like(unit)
    first = jnp.zeros_like(unit)
    for shift, part in enumerate(parts):
        spot = (place + shift) % radix
        last = last + decayed(unit, group * (radix - 1 - spot)) * part[0]
        first = first + decayed(unit, group * spot) * part[1]
    return last, first


def join_kernel(level, rows, place, theta, *refs):
    parts, result = refs[:-1], refs[-1]
    last, first = join(rows * theta[...], place[0], parts, level)
    result[0] = last
    result[1] = first


def join_level(level, rows, place, theta, parts):
    vmem, smem = pl.BlockSpec(memory_space=pltpu.VMEM), pl.BlockSpec(memory_space=pltpu.SMEM)
    return pl.pallas_call(
        functools.partial(join_kernel, level, rows),
        in_specs=[smem, vmem] + [vmem] * len(parts),
        out_specs=vmem,
        out_shape=jax.ShapeDtypeStruct(parts[0].shape, F32),
        compiler_params=params(8),
        name="join",
    )(place, theta, *parts)


def entering(theta, rows, me, blocks, levels):
    unit = rows * theta
    above = jnp.zeros_like(theta)
    below = jnp.zeros_like(theta)
    for level, parts in enumerate(levels):
        radix, group = RADICES[level], math.prod(RADICES[:level])
        spot_here, inside = (me // group) % radix, me % group
        for shift in range(1, radix):
            spot = (spot_here + shift) % radix
            over = jnp.maximum(group * (spot_here - 1 - spot), 0) + inside
            under = jnp.maximum(group * (spot - spot_here - 1), 0) + group - 1 - inside
            above = above + jnp.where(spot < spot_here, decayed(unit, over), 0.0) * parts[shift][0]
            below = below + jnp.where(spot > spot_here, decayed(unit, under), 0.0) * parts[shift][1]
    last, first = join(unit, me, levels[-1], len(levels) - 1)
    span = jnp.exp(-theta * (rows * blocks + 1))
    wall = jnp.exp(-theta) / (1.0 - span * span)
    above = above + decayed(unit, me) * wall * (span * last - first)
    below = below + decayed(unit, blocks - 1 - me) * wall * (span * first - last)
    return above, below


def solve_kernel(blocks, place, theta, modal, ratio, scale, mix_high, mix_low, *refs):
    count = sum(RADICES)
    parts, (result, down, up) = refs[:count], refs[count:]
    rows, layers, width = modal.shape
    step = result.shape[1]
    decay = ratio[...]

    @pl.when(pl.program_id(0) == 0)
    def _():
        levels, at = [], 0
        for radix in RADICES:
            levels.append(parts[at : at + radix])
            at += radix
        above, below = entering(theta[...], rows, place[0], blocks, levels)
        up[...] = below

        def forth(row, value):
            value = decay * value + modal[row]
            down[row] = value
            return value

        lax.fori_loop(0, rows, forth, above, unroll=8)

    base = rows - step * (pl.program_id(0) + 1)
    beyond, factor = up[...], scale[...]
    solved = [None] * step
    for row in range(step - 1, -1, -1):
        value = decay * beyond
        beyond = modal[base + row] + value
        solved[row] = factor * (down[base + row] + value)
    up[...] = beyond
    for t in range(step // 8):
        high, low = split(jnp.stack(solved[8 * t : 8 * t + 8]).reshape(8 * layers, width))
        mixed = dot(mix_high[...], high) + dot(mix_low[...], high) + dot(mix_high[...], low)
        result[:, 8 * t : 8 * t + 8, :] = mixed.reshape(layers, 8, width)


def solve(place, theta, modal, ratio, scale, mix_high, mix_low, parts, blocks):
    rows, layers, width = modal.shape
    step = 16
    whole = pl.BlockSpec(mix_high.shape, lambda i: (0, 0))
    field = pl.BlockSpec((layers, width), lambda i: (0, 0))
    return pl.pallas_call(
        functools.partial(solve_kernel, blocks),
        grid=(rows // step,),
        in_specs=[
            pl.BlockSpec(memory_space=pltpu.SMEM),
            field,
            pl.BlockSpec((rows, layers, width), lambda i: (0, 0, 0)),
            field,
            field,
            whole,
            whole,
        ]
        + [pl.BlockSpec((2, layers, width), lambda i: (0, 0, 0))] * len(parts),
        out_specs=pl.BlockSpec((layers, step, width), lambda i: (0, rows // step - 1 - i, 0)),
        out_shape=jax.ShapeDtypeStruct((layers, rows, width), F32),
        scratch_shapes=[pltpu.VMEM((rows, layers, width), F32), pltpu.VMEM((layers, width), F32)],
        compiler_params=params(16),
        name="solve",
    )(place, theta, modal, ratio, scale, mix_high, mix_low, *parts)


def inverse_kernel(source, table_high, table_low, result, high, low, held, sems):
    shards, lines, width = source.shape
    width //= 2
    index = pl.program_id(0)

    @pl.when(index == 0)
    def _():
        for part in range(shards):
            column = slice(part * width, (part + 1) * width)
            for parity in range(2):
                line = slice(parity * lines, (parity + 1) * lines)
                high[line, column], low[line, column] = split(source[part, :, parity * width : (parity + 1) * width])

    value = three_dots(high[...], low[...], table_high[...], table_low[...])
    step = value.shape[1]
    count = result.shape[1] // step
    odd, even = value[:lines] * alternating((1, step)), value[lines:]
    held[index] = odd + even
    mirror = odd - even
    order = LANES - 1 - lax.broadcasted_iota(jnp.int32, (lines, LANES), 1)
    for part in range(step // LANES):
        block = mirror[:, step - LANES * (part + 1) : step - LANES * part]
        held[count - 1 - index, :, LANES * part : LANES * (part + 1)] = jnp.take_along_axis(block, order, axis=1)

    def copy(block):
        column = pl.ds(pl.multiple_of(block * step, step), step)
        return pltpu.make_async_copy(held.at[block], result.at[:, column], sems.at[block])

    copy(index).start()
    copy(count - 1 - index).start()

    @pl.when(index == pl.num_programs(0) - 1)
    def _():
        for block in range(count):
            copy(block).wait()


def inverse(source, table_high, table_low):
    shards, lines, width = source.shape
    depth = shards * width // 2
    step = 256
    count = 2 * depth // step
    column = pl.BlockSpec((depth, step), lambda i: (0, i))
    return pl.pallas_call(
        inverse_kernel,
        grid=(depth // step,),
        in_specs=[pl.BlockSpec(source.shape, lambda i: (0, 0, 0)), column, column],
        out_specs=pl.BlockSpec(memory_space=pltpu.HBM),
        out_shape=jax.ShapeDtypeStruct((lines, 2 * depth), F32),
        scratch_shapes=[pltpu.VMEM((2 * lines, depth), BF16)] * 2
        + [pltpu.VMEM((count, lines, step), F32), pltpu.SemaphoreType.DMA((count,))],
        compiler_params=params(24),
        name="inverse",
    )(source, table_high, table_low)


def on_device(q_prev, q_now, psi_now, layers_to_modes, modes_to_layers, stretch):
    layer_count, row_count, col_count = q_prev.shape
    blocks = lax.axis_size("row")
    shards = lax.axis_size("layer")
    me = lax.axis_index("row")
    table_high, table_low = (jnp.asarray(value) for value in half_table(col_count))
    eigen = jnp.asarray(column_eigen(col_count, shards))
    place = me.astype(jnp.int32).reshape(1)
    shard = lax.axis_index("layer").astype(jnp.int32).reshape(1)

    initial, last = rims(q_prev, q_now, psi_now)
    pairs = [(i, i + 1) for i in range(blocks - 1)]
    top = lax.ppermute(last, "row", pairs)
    bottom = lax.ppermute(initial, "row", [(j, i) for i, j in pairs])
    theta, ratio, scale, *mixes = prepare(shard, eigen, stretch, layers_to_modes, modes_to_layers)
    q_next, spectrum = step_forward(place, q_prev, q_now, psi_now, top, bottom, table_high, table_low, shards, blocks)
    stacked = lax.all_to_all(spectrum, "layer", split_axis=0, concat_axis=0, tiled=True)
    stacked = stacked.reshape(shards * layer_count, row_count, -1)
    modal, total = project(stacked, mixes[0], mixes[1], ratio)
    parts = []
    for level in range(len(RADICES)):
        group = [total] + exchange(total, level, blocks)
        parts.extend(group)
        if level + 1 < len(RADICES):
            total = join_level(level, row_count, place, theta, group)
    layered = solve(place, theta, modal, ratio, scale, mixes[2], mixes[3], parts, blocks)
    layered = layered.reshape(shards, layer_count * row_count, -1)
    returned = lax.all_to_all(layered, "layer", split_axis=0, concat_axis=0, tiled=True)
    psi_next = inverse(returned, table_high, table_low)
    return (q_next, psi_next.reshape(q_prev.shape))


def solution(mesh):
    return jax.shard_map(
        on_device,
        mesh=mesh,
        in_specs=(
            P("layer", "row", None),
            P("layer", "row", None),
            P("layer", "row", None),
            P(),
            P(),
            P(),
        ),
        out_specs=(P("layer", "row", None), P("layer", "row", None)),
        check_vma=False,
    )
```

```python
import functools
import math

import jax
import jax.numpy as jnp
import ml_dtypes
import numpy as np
from jax import lax
from jax.experimental import pallas as pl
from jax.experimental.pallas import tpu as pltpu
from jax.sharding import PartitionSpec as P

TIME_STEP = 0.1
VISCOSITY = 0.02
F32 = jnp.float32
BF16 = jnp.bfloat16
LANES = 128
LAG = 2
INNER_LIMIT = 46
OUTER_LIMIT = 24


def params(megabytes):
    return pltpu.CompilerParams(vmem_limit_bytes=megabytes << 20)


def half_table(length):
    positions = np.arange(1, length // 2 + 1, dtype=np.int64)
    product = (2 * positions[:, None] * positions[None, :]) % (2 * (length + 1))
    table = np.sin(product.astype(np.float64) * (math.pi / (length + 1)))
    high = table.astype(np.float32).astype(ml_dtypes.bfloat16)
    low = (table - high.astype(np.float64)).astype(np.float32).astype(ml_dtypes.bfloat16)
    return high, low


def column_eigen(length, shards):
    positions = np.arange(1, length // 2 + 1, dtype=np.float64)
    waves = np.stack([length + 1 - 2 * positions, 2 * positions])
    eigen = 4.0 * np.sin(waves * (math.pi / (2 * (length + 1)))) ** 2
    eigen = eigen.astype(np.float32).reshape(2, shards, -1)
    return np.concatenate([eigen[0], eigen[1]], axis=1)


def split(value):
    high = value.astype(BF16)
    low = (value - high.astype(F32)).astype(BF16)
    return high, low


def dot(left, right):
    return jnp.dot(left, right, preferred_element_type=F32)


def three_dots(high, low, table_high, table_low):
    return dot(high, table_high) + dot(low, table_high) + dot(high, table_low)


def alternating(shape):
    lane = lax.broadcasted_iota(jnp.int32, shape, 1)
    return jnp.where(lane % 2 == 0, 1.0, -1.0).astype(F32)


def vmem():
    return pl.BlockSpec(memory_space=pltpu.VMEM)


def smem():
    return pl.BlockSpec(memory_space=pltpu.SMEM)


def rim_kernel(prev_first, now_first, psi_first, prev_last, now_last, psi_last, initial, last):
    rows = prev_last.shape[1]
    initial[:, 0:1] = psi_first[:, 0:1]
    initial[:, 1:2] = now_first[:, 0:1]
    initial[:, 2:4] = prev_first[:, 0:2]
    last[:, 0:1] = psi_last[:, rows - 1 :]
    last[:, 1:2] = now_last[:, rows - 1 :]
    last[:, 2:4] = prev_last[:, rows - 2 :]


def rims(q_prev, q_now, psi_now):
    layers, rows, cols = q_prev.shape
    first = pl.BlockSpec((layers, 8, cols), lambda i: (0, 0, 0))
    final = pl.BlockSpec((layers, 8, cols), lambda i: (0, rows // 8 - 1, 0))
    rim = jax.ShapeDtypeStruct((layers, 4, cols), F32)
    whole = pl.BlockSpec(rim.shape, lambda i: (0, 0, 0))
    return pl.pallas_call(
        rim_kernel,
        grid=(1,),
        in_specs=[first, first, first, final, final, final],
        out_specs=[whole, whole],
        out_shape=[rim, rim],
        compiler_params=params(62),
        name="rims",
    )(q_prev, q_now, psi_now, q_prev, q_now, psi_now)


def shift_columns(source, to_east, to_west):
    count, rows, width = source.shape
    lane = lax.broadcasted_iota(jnp.int32, (rows, width), 1)
    east, west = {count: 0.0}, {-1: 0.0}

    def store(c):
        to_east[c] = jnp.where(lane == width - 1, east[c + 1], east[c])
        to_west[c] = jnp.where(lane == 0, west[c - 1], west[c])

    for c in range(count + LAG):
        if c < count:
            value = source[c]
            east[c] = pltpu.roll(value, width - 1, 1)
            west[c] = pltpu.roll(value, 1, 1)
        if c >= LAG:
            store(c - LAG)


def advance(fields, segments, rows, store):
    p, z, ze, zw, q, qe, qw = fields
    count, _, width = p.shape
    lane = lax.broadcasted_iota(jnp.int32, (rows, width), 1)
    third = -2.0 * TIME_STEP / 12.0
    drag = -2.0 * TIME_STEP * VISCOSITY
    middle = {}
    east = {(n, count): 0.0 for n in range(len(segments))}
    west = {(n, -1): 0.0 for n in range(len(segments))}

    def tendency(n, c):
        start, wall = segments[n]

        def here(ext, row=0):
            return ext[c, start + row : start + row + rows, :]

        pn, pc, ps = here(p, -1), here(p), here(p, 1)
        zn, zc, zs = here(z, -1), here(z), here(z, 1)
        zne, zce, zse = here(ze, -1), here(ze), here(ze, 1)
        znw, zcw, zsw = here(zw, -1), here(zw), here(zw, 1)
        qc = here(q)
        near = here(q, -1) + here(q, 1)
        far = here(q, -2) + here(q, 2)
        down = zs - zn
        beside = 2.0 * near - 8.0 * qc
        from_east = pc * ((zsw - znw) + down) + ps * (zsw - zc) + pn * (zc - znw)
        from_west = ps * (zc - zse) + pn * (zne - zc) - pc * ((zse - zne) + down)
        from_east = third * from_east + drag * (beside + here(qe))
        from_west = third * from_west + drag * (beside + here(qw))
        east[n, c] = pltpu.roll(from_east, width - 1, 1)
        west[n, c] = pltpu.roll(from_west, 1, 1)
        across = zce - zcw
        own = pn * (across + (zne - znw)) - ps * (across + (zse - zsw))
        bulk = far - 8.0 * near + 20.0 * qc
        if wall is not None:
            bulk = bulk - wall * qc
        if c == 0:
            bulk = bulk - jnp.where(lane == 0, qc, 0.0)
        if c == count - 1:
            bulk = bulk - jnp.where(lane == width - 1, qc, 0.0)
        middle[n, c] = qc + third * own + drag * bulk

    def finish(n, c):
        value = middle[n, c] + jnp.where(lane == width - 1, east[n, c + 1], east[n, c])
        store(n, c, value + jnp.where(lane == 0, west[n, c - 1], west[n, c]))

    for c in range(count + LAG):
        for n in range(len(segments)):
            if c < count:
                tendency(n, c)
            if c >= LAG:
                finish(n, c - LAG)


def fold_columns(count, rows, read, write):
    lane = lax.broadcasted_iota(jnp.int32, (rows, LANES), 1)
    order = LANES - 1 - lane
    sign = alternating((rows, LANES))
    pairs = {}
    for c in range(count // 2 + LAG):
        if c < count // 2:
            pairs[c] = read(c), jnp.take_along_axis(read(count - 1 - c), order, axis=1)
        if c >= LAG:
            lower, upper = pairs[c - LAG]
            write(c - LAG, (lower + upper) * sign, lower - upper)


def inner_kernel(prev, now, psi, table_high_in, table_low_in, q_out, high, low, rim, near, table_high, table_low, *scratch):
    fields, q_held, p, z, ze, zw, q, qe, qw, sems, q_sems, table_sems = scratch
    layers, rows, cols = prev.shape
    inner = rows - 16
    layer = pl.program_id(0)

    def load(index, which):
        source = (psi, now, prev)[which]
        slot = index % 2
        return pltpu.make_async_copy(source.at[index], fields.at[slot, which], sems.at[slot, which])

    def save(index):
        return pltpu.make_async_copy(
            q_held.at[index, pl.ds(8, inner)], q_out.at[index, pl.ds(8, inner)], q_sems.at[index]
        )

    tables = [
        pltpu.make_async_copy(table_high_in, table_high, table_sems.at[0]),
        pltpu.make_async_copy(table_low_in, table_low, table_sems.at[1]),
    ]

    @pl.when(layer == 0)
    def _():
        for index in range(2):
            for which in range(3):
                load(index, which).start()

    for which in range(3):
        load(layer, which).wait()
    for which, ext in enumerate((p, z, q)):
        for c in range(ext.shape[0]):
            ext[c, 8 : 8 + rows, :] = fields[layer % 2, which, :, LANES * c : LANES * (c + 1)]
        near[which, layer, 0:4] = fields[layer % 2, which, 0:4]
        near[which, layer, 4:8] = fields[layer % 2, which, rows - 4 :]

    @pl.when(layer + 2 < layers)
    def _():
        for which in range(3):
            load(layer + 2, which).start()

    @pl.when(layer == layers - 2)
    def _():
        for table in tables:
            table.start()

    shift_columns(z, ze, zw)
    shift_columns(q, qe, qw)

    def store(n, c, value):
        q_held[layer, :, LANES * c : LANES * (c + 1)] = value

    advance((p, z, ze, zw, q, qe, qw), [(8, None)], rows, store)
    save(layer).start()
    rim[layer, 0:8] = q_held[layer, 0:8]
    rim[layer, 8:16] = q_held[layer, rows - 8 :]

    def read(c):
        return q_held[layer, 8 : 8 + inner, LANES * c : LANES * (c + 1)]

    def write(c, *folds):
        for parity, value in enumerate(folds):
            line = pl.ds(pl.multiple_of((parity * layers + layer) * inner, inner), inner)
            column = slice(LANES * c, LANES * (c + 1))
            high[line, column], low[line, column] = split(value)

    fold_columns(cols // LANES, inner, read, write)

    @pl.when(layer == layers - 1)
    def _():
        for index in range(layers):
            save(index).wait()
        for table in tables:
            table.wait()


def inner_step(q_prev, q_now, psi_now, table_high, table_low):
    layers, rows, cols = q_prev.shape
    depth = cols // 2
    hbm = pl.BlockSpec(memory_space=pltpu.HBM)
    lines = jax.ShapeDtypeStruct((2 * layers * (rows - 16), depth), BF16)
    table = jax.ShapeDtypeStruct((depth, depth), BF16)
    return pl.pallas_call(
        inner_kernel,
        grid=(layers,),
        in_specs=[hbm] * 5,
        out_specs=[hbm] + [vmem()] * 6,
        out_shape=[
            jax.ShapeDtypeStruct(q_prev.shape, F32),
            lines,
            lines,
            jax.ShapeDtypeStruct((layers, 16, cols), F32),
            jax.ShapeDtypeStruct((3, layers, 8, cols), F32),
            table,
            table,
        ],
        scratch_shapes=[pltpu.VMEM((2, 3, rows, cols), F32), pltpu.VMEM((layers, rows, cols), F32)]
        + [pltpu.VMEM((cols // LANES, rows + 16, LANES), F32)] * 7
        + [
            pltpu.SemaphoreType.DMA((2, 3)),
            pltpu.SemaphoreType.DMA((layers,)),
            pltpu.SemaphoreType.DMA((2,)),
        ],
        compiler_params=params(INNER_LIMIT),
        cost_estimate=pl.CostEstimate(flops=60 * layers * rows * cols, bytes_accessed=12 << 20, transcendentals=0),
        name="inner_step",
    )(q_prev, q_now, psi_now, table_high, table_low)


def outer_kernel(blocks, place, top, bottom, high_in, low_in, rim, near, table_high, table_low, q_in, q_out, spectrum, *scratch):
    q_rim, p, z, ze, zw, q, qe, qw, high, low, held, q_sems, sems = scratch
    layers, _, cols = rim.shape
    shards, lines, width = held.shape
    width //= 2
    rows = lines // layers
    inner = rows - 16

    for n in range(layers):
        first, last = 8 + 32 * n, 24 + 32 * n
        for which, (ext, row, size) in enumerate(((p, 0, 1), (z, 1, 1), (q, 2, 2))):
            for c in range(cols // LANES):
                column = slice(LANES * c, LANES * (c + 1))
                ext[c, first - size : first, :] = top[n, row : row + size, column]
                ext[c, first : first + 4, :] = near[which, n, 0:4, column]
                ext[c, last + 4 : last + 8, :] = near[which, n, 4:8, column]
                ext[c, last + 8 : last + 8 + size, :] = bottom[n, row : row + size, column]
    shift_columns(z, ze, zw)
    shift_columns(q, qe, qw)
    row = lax.broadcasted_iota(jnp.int32, (8, LANES), 0)
    wall_above = jnp.where(row == jnp.where(place[0] == 0, 0, -1), 1.0, 0.0).astype(F32)
    wall_below = jnp.where(row == jnp.where(place[0] == blocks - 1, 7, -1), 1.0, 0.0).astype(F32)
    segments = []
    for n in range(layers):
        segments += [(8 + 32 * n, wall_above), (24 + 32 * n, wall_below)]

    def store(n, c, value):
        at, column = slice(8 * (n % 2), 8 * (n % 2) + 8), slice(LANES * c, LANES * (c + 1))
        fresh = row >= 6 if n % 2 else row < 2
        q_rim[n // 2, at, column] = jnp.where(fresh, value, rim[n // 2, at, column])

    advance((p, z, ze, zw, q, qe, qw), segments, 8, store)

    def save(n, edge):
        source = q_rim.at[n, pl.ds(8 * edge, 8)]
        return pltpu.make_async_copy(source, q_out.at[n, pl.ds((rows - 8) * edge, 8)], q_sems.at[n, edge])

    for n in range(layers):
        for edge in range(2):
            save(n, edge).start()

    for block in range(2 * layers):
        line = slice(block * rows, block * rows + inner)
        high[line, :] = high_in[block * inner : (block + 1) * inner, :]
        low[line, :] = low_in[block * inner : (block + 1) * inner, :]
    for n in range(layers):

        def read(c):
            return q_rim[n, :, LANES * c : LANES * (c + 1)]

        def write(c, *folds):
            for parity, value in enumerate(folds):
                start = (parity * layers + n) * rows + inner
                column = slice(LANES * c, LANES * (c + 1))
                high[start : start + 16, column], low[start : start + 16, column] = split(value)

        fold_columns(cols // LANES, 16, read, write)

    def send(step):
        block = pl.ds(2 * step, 2)
        return pltpu.make_async_copy(held.at[block], spectrum.at[block], sems.at[step])

    def columns(step, carry):
        span = pl.ds(pl.multiple_of(step * 2 * width, 2 * width), 2 * width)
        value = three_dots(high[...], low[...], table_high[:, span], table_low[:, span])
        for part in range(2):
            column = slice(part * width, (part + 1) * width)
            for parity in range(2):
                lane = slice(parity * width, (parity + 1) * width)
                for n in range(layers):
                    start, to = (parity * layers + n) * rows, n * rows
                    held[2 * step + part, to + 8 : to + 8 + inner, lane] = value[start : start + inner, column]
                    held[2 * step + part, to : to + 8, lane] = value[start + inner : start + inner + 8, column]
                    held[2 * step + part, to + rows - 8 : to + rows, lane] = value[start + rows - 8 : start + rows, column]
        send(step).start()
        return carry

    lax.fori_loop(0, shards // 2, columns, 0)
    for n in range(layers):
        for edge in range(2):
            save(n, edge).wait()
    for step in range(shards // 2):
        send(step).wait()


def outer_step(place, top, bottom, high, low, rim, near, table_high, table_low, q_next, shards, blocks):
    layers, rows, cols = q_next.shape
    depth = cols // 2
    lines = layers * rows
    width = depth // shards
    hbm = pl.BlockSpec(memory_space=pltpu.HBM)
    return pl.pallas_call(
        functools.partial(outer_kernel, blocks),
        in_specs=[smem()] + [vmem()] * 8 + [hbm],
        out_specs=[hbm, hbm],
        out_shape=[
            jax.ShapeDtypeStruct(q_next.shape, F32),
            jax.ShapeDtypeStruct((shards, lines, 2 * width), F32),
        ],
        input_output_aliases={9: 0},
        scratch_shapes=[pltpu.VMEM((layers, 16, cols), F32)]
        + [pltpu.VMEM((cols // LANES, 32 * layers + 8, LANES), F32)] * 7
        + [pltpu.VMEM((2 * lines, depth), BF16)] * 2
        + [
            pltpu.VMEM((shards, lines, 2 * width), F32),
            pltpu.SemaphoreType.DMA((layers, 2)),
            pltpu.SemaphoreType.DMA((shards // 2,)),
        ],
        compiler_params=params(OUTER_LIMIT),
        cost_estimate=pl.CostEstimate(flops=12 * lines * depth * depth, bytes_accessed=4 << 20, transcendentals=0),
        name="outer_step",
    )(place, top, bottom, high, low, rim, near, table_high, table_low, q_next)


def prepare_kernel(shard, eigen, stretch, to_modes, to_layers, theta, ratio, scale, in_high, in_low, out_high, out_low):
    modes, width = theta.shape
    wave = eigen[pl.ds(shard[0], 1), :]
    for mode in range(modes):
        theta[mode : mode + 1, :] = wave + stretch[mode]
    shift = theta[...]
    half = 0.5 * jnp.sqrt(shift)
    angle = 2.0 * jnp.log1p(half + half * half / (1.0 + jnp.sqrt(1.0 + half * half)))
    theta[...] = angle
    ratio[...] = jnp.exp(-angle)
    scale[...] = (-2.0 / (width * eigen.shape[0] + 1)) / jnp.sqrt(shift * (4.0 + shift))

    size = 8 * modes
    line = lax.broadcasted_iota(jnp.int32, (size, modes), 0)
    index = lax.broadcasted_iota(jnp.int32, (size, modes), 1)
    by_layer = (line // 8 == index).astype(F32)
    by_mode = (line % modes == index).astype(F32)
    down = lax.broadcasted_iota(jnp.int32, (size, size), 0)
    along = lax.broadcasted_iota(jnp.int32, (size, size), 1)

    def exact(left, right, sides):
        return lax.dot_general(
            left, right, ((sides, ((), ()))), precision=lax.Precision.HIGHEST, preferred_element_type=F32
        )

    spread = exact(exact(by_mode, to_modes[...], ((1,), (0,))), by_layer, ((1,), (1,)))
    in_high[...], in_low[...] = split(jnp.where(down // modes == along % 8, spread, 0.0))
    spread = exact(exact(by_layer, to_layers[...], ((1,), (0,))), by_mode, ((1,), (1,)))
    out_high[...], out_low[...] = split(jnp.where(down % 8 == along // modes, spread, 0.0))


def prepare(shard, eigen, stretch, to_modes, to_layers):
    modes, width = stretch.shape[0], eigen.shape[1]
    field = jax.ShapeDtypeStruct((modes, width), F32)
    mix = jax.ShapeDtypeStruct((8 * modes, 8 * modes), BF16)
    return pl.pallas_call(
        prepare_kernel,
        in_specs=[smem(), vmem(), smem(), vmem(), vmem()],
        out_specs=[vmem()] * 7,
        out_shape=[field, field, field, mix, mix, mix, mix],
        compiler_params=params(8),
        name="prepare",
    )(shard, eigen, stretch, to_modes, to_layers)


def project_kernel(source, mix_high, mix_low, ratio, modal, ends):
    layers, rows, width = source.shape
    decay = ratio[...]

    def tile(t, sums):
        last, first, scale = sums
        at = pl.ds(pl.multiple_of(8 * t, 8), 8)
        high, low = split(source[:, at, :].reshape(8 * layers, width))
        mixed = dot(mix_high[...], high) + dot(mix_low[...], high) + dot(mix_high[...], low)
        block = mixed.reshape(8, layers, width)
        modal[at] = block
        for row in range(8):
            last = decay * last + block[row]
            first = first + scale * block[row]
            scale = scale * decay
        return last, first, scale

    zeros = jnp.zeros((layers, width), F32)
    last, first, _ = lax.fori_loop(0, rows // 8, tile, (zeros, zeros, zeros + 1.0), unroll=2)
    ends[0] = last
    ends[1] = first


def project(stacked, mix_high, mix_low, ratio):
    layers, rows, width = stacked.shape
    return pl.pallas_call(
        project_kernel,
        in_specs=[vmem()] * 4,
        out_specs=[vmem()] * 2,
        out_shape=[
            jax.ShapeDtypeStruct((rows, layers, width), F32),
            jax.ShapeDtypeStruct((2, layers, width), F32),
        ],
        compiler_params=params(8),
        name="project",
    )(stacked, mix_high, mix_low, ratio)


RADICES = (2, 4, 4)


def exchange(total, level, blocks):
    radix, group = RADICES[level], math.prod(RADICES[:level])
    parts = []
    for shift in range(1, radix):
        pairs = []
        for target in range(blocks):
            spot = (target // group) % radix
            pairs.append((target + ((spot + shift) % radix - spot) * group, target))
        parts.append(lax.ppermute(total, "row", pairs))
    return parts


def decayed(unit, count):
    return jnp.exp(-unit * count.astype(F32))


def join(unit, me, parts, level):
    radix, group = RADICES[level], math.prod(RADICES[:level])
    place = (me // group) % radix
    last = jnp.zeros_like(unit)
    first = jnp.zeros_like(unit)
    for shift, part in enumerate(parts):
        spot = (place + shift) % radix
        last = last + decayed(unit, group * (radix - 1 - spot)) * part[0]
        first = first + decayed(unit, group * spot) * part[1]
    return last, first


def join_kernel(level, rows, place, theta, *refs):
    parts, result = refs[:-1], refs[-1]
    last, first = join(rows * theta[...], place[0], parts, level)
    result[0] = last
    result[1] = first


def join_level(level, rows, place, theta, parts):
    return pl.pallas_call(
        functools.partial(join_kernel, level, rows),
        in_specs=[smem(), vmem()] + [vmem()] * len(parts),
        out_specs=vmem(),
        out_shape=jax.ShapeDtypeStruct(parts[0].shape, F32),
        compiler_params=params(8),
        name="join",
    )(place, theta, *parts)


def entering(theta, rows, me, blocks, levels):
    unit = rows * theta
    above = jnp.zeros_like(theta)
    below = jnp.zeros_like(theta)
    for level, parts in enumerate(levels):
        radix, group = RADICES[level], math.prod(RADICES[:level])
        spot_here, inside = (me // group) % radix, me % group
        for shift in range(1, radix):
            spot = (spot_here + shift) % radix
            over = jnp.maximum(group * (spot_here - 1 - spot), 0) + inside
            under = jnp.maximum(group * (spot - spot_here - 1), 0) + group - 1 - inside
            above = above + jnp.where(spot < spot_here, decayed(unit, over), 0.0) * parts[shift][0]
            below = below + jnp.where(spot > spot_here, decayed(unit, under), 0.0) * parts[shift][1]
    last, first = join(unit, me, levels[-1], len(levels) - 1)
    span = jnp.exp(-theta * (rows * blocks + 1))
    wall = jnp.exp(-theta) / (1.0 - span * span)
    above = above + decayed(unit, me) * wall * (span * last - first)
    below = below + decayed(unit, blocks - 1 - me) * wall * (span * first - last)
    return above, below


def solve_kernel(blocks, place, theta, modal, ratio, scale, mix_high, mix_low, *refs):
    count = sum(RADICES)
    parts, (result, down) = refs[:count], refs[count:]
    rows, layers, width = modal.shape
    decay, factor = ratio[...], scale[...]
    levels, at = [], 0
    for radix in RADICES:
        levels.append(parts[at : at + radix])
        at += radix
    above, below = entering(theta[...], rows, place[0], blocks, levels)

    def forth(row, value):
        value = decay * value + modal[row]
        down[row] = value
        return value

    lax.fori_loop(0, rows, forth, above, unroll=8)

    def tile(step, beyond):
        base = pl.multiple_of(rows - 8 * (step + 1), 8)
        solved = [None] * 8
        for row in range(7, -1, -1):
            value = decay * beyond
            beyond = modal[base + row] + value
            solved[row] = factor * (down[base + row] + value)
        high, low = split(jnp.stack(solved).reshape(8 * layers, width))
        mixed = dot(mix_high[...], high) + dot(mix_low[...], high) + dot(mix_high[...], low)
        result[:, pl.ds(base, 8), :] = mixed.reshape(layers, 8, width)
        return beyond

    lax.fori_loop(0, rows // 8, tile, below, unroll=2)


def solve(place, theta, modal, ratio, scale, mix_high, mix_low, parts, blocks):
    rows, layers, width = modal.shape
    return pl.pallas_call(
        functools.partial(solve_kernel, blocks),
        in_specs=[smem()] + [vmem()] * (6 + len(parts)),
        out_specs=vmem(),
        out_shape=jax.ShapeDtypeStruct((layers, rows, width), F32),
        scratch_shapes=[pltpu.VMEM((rows, layers, width), F32)],
        compiler_params=params(12),
        name="solve",
    )(place, theta, modal, ratio, scale, mix_high, mix_low, *parts)


def inverse_kernel(source, table_high, table_low, result, high, low, held, sems):
    shards, lines, width = source.shape
    width //= 2
    for part in range(shards):
        column = slice(part * width, (part + 1) * width)
        for parity in range(2):
            line = slice(parity * lines, (parity + 1) * lines)
            high[line, column], low[line, column] = split(source[part, :, parity * width : (parity + 1) * width])

    count, _, step = held.shape
    order = LANES - 1 - lax.broadcasted_iota(jnp.int32, (lines, LANES), 1)
    sign = alternating((1, step))

    def copy(block):
        column = pl.ds(block * step, step)
        return pltpu.make_async_copy(held.at[block], result.at[:, column], sems.at[block])

    def columns(index):
        span = slice(index * step, (index + 1) * step)
        value = three_dots(high[...], low[...], table_high[:, span], table_low[:, span])
        odd, even = value[:lines] * sign, value[lines:]
        held[index] = odd + even
        copy(index).start()
        mirror = odd - even
        for part in range(step // LANES):
            block = mirror[:, step - LANES * (part + 1) : step - LANES * part]
            held[count - 1 - index, :, LANES * part : LANES * (part + 1)] = jnp.take_along_axis(block, order, axis=1)
        copy(count - 1 - index).start()

    for index in range(count // 2):
        columns(index)
    for block in range(count):
        copy(block).wait()


def inverse(source, table_high, table_low):
    shards, lines, width = source.shape
    depth = shards * width // 2
    step = 256
    count = 2 * depth // step
    return pl.pallas_call(
        inverse_kernel,
        in_specs=[vmem()] * 3,
        out_specs=pl.BlockSpec(memory_space=pltpu.HBM),
        out_shape=jax.ShapeDtypeStruct((lines, 2 * depth), F32),
        scratch_shapes=[pltpu.VMEM((2 * lines, depth), BF16)] * 2
        + [pltpu.VMEM((count, lines, step), F32), pltpu.SemaphoreType.DMA((count,))],
        compiler_params=params(14),
        name="inverse",
    )(source, table_high, table_low)


def on_device(q_prev, q_now, psi_now, layers_to_modes, modes_to_layers, stretch):
    layer_count, row_count, col_count = q_prev.shape
    blocks = lax.axis_size("row")
    shards = lax.axis_size("layer")
    me = lax.axis_index("row")
    table_high, table_low = (jnp.asarray(value) for value in half_table(col_count))
    eigen = jnp.asarray(column_eigen(col_count, shards))
    place = me.astype(jnp.int32).reshape(1)
    shard = lax.axis_index("layer").astype(jnp.int32).reshape(1)

    initial, last = rims(q_prev, q_now, psi_now)
    pairs = [(i, i + 1) for i in range(blocks - 1)]
    top = lax.ppermute(last, "row", pairs)
    bottom = lax.ppermute(initial, "row", [(j, i) for i, j in pairs])
    theta, ratio, scale, *mixes = prepare(shard, eigen, stretch, layers_to_modes, modes_to_layers)
    q_next, *folded, table_high, table_low = inner_step(q_prev, q_now, psi_now, table_high, table_low)
    q_next, spectrum = outer_step(place, top, bottom, *folded, table_high, table_low, q_next, shards, blocks)
    stacked = lax.all_to_all(spectrum, "layer", split_axis=0, concat_axis=0, tiled=True)
    stacked = stacked.reshape(shards * layer_count, row_count, -1)
    modal, total = project(stacked, mixes[0], mixes[1], ratio)
    parts = []
    for level in range(len(RADICES)):
        group = [total] + exchange(total, level, blocks)
        parts.extend(group)
        if level + 1 < len(RADICES):
            total = join_level(level, row_count, place, theta, group)
    layered = solve(place, theta, modal, ratio, scale, mixes[2], mixes[3], parts, blocks)
    layered = layered.reshape(shards, layer_count * row_count, -1)
    returned = lax.all_to_all(layered, "layer", split_axis=0, concat_axis=0, tiled=True)
    psi_next = inverse(returned, table_high, table_low)
    return (q_next, psi_next.reshape(q_prev.shape))


def solution(mesh):
    return jax.shard_map(
        on_device,
        mesh=mesh,
        in_specs=(
            P("layer", "row", None),
            P("layer", "row", None),
            P("layer", "row", None),
            P(),
            P(),
            P(),
        ),
        out_specs=(P("layer", "row", None), P("layer", "row", None)),
        check_vma=False,
    )
```

```python
import functools
import math

import jax
import jax.numpy as jnp
import ml_dtypes
import numpy as np
from jax import lax
from jax.experimental import pallas as pl
from jax.experimental.pallas import tpu as pltpu
from jax.sharding import PartitionSpec as P

TIME_STEP = 0.1
VISCOSITY = 0.02
F32 = jnp.float32
BF16 = jnp.bfloat16
LANES = 128
LAG = 2
INNER_LIMIT = 46
OUTER_LIMIT = 24


def params(megabytes):
    return pltpu.CompilerParams(vmem_limit_bytes=megabytes << 20)


def half_table(length):
    positions = np.arange(1, length // 2 + 1, dtype=np.int64)
    product = (2 * positions[:, None] * positions[None, :]) % (2 * (length + 1))
    table = np.sin(product.astype(np.float64) * (math.pi / (length + 1)))
    high = table.astype(np.float32).astype(ml_dtypes.bfloat16)
    low = (table - high.astype(np.float64)).astype(np.float32).astype(ml_dtypes.bfloat16)
    return high, low


def column_eigen(length, shards):
    positions = np.arange(1, length // 2 + 1, dtype=np.float64)
    waves = np.stack([length + 1 - 2 * positions, 2 * positions])
    eigen = 4.0 * np.sin(waves * (math.pi / (2 * (length + 1)))) ** 2
    eigen = eigen.astype(np.float32).reshape(2, shards, -1)
    return np.concatenate([eigen[0], eigen[1]], axis=1)


def split(value):
    high = value.astype(BF16)
    low = (value - high.astype(F32)).astype(BF16)
    return high, low


def dot(left, right):
    return jnp.dot(left, right, preferred_element_type=F32)


def three_dots(high, low, table_high, table_low):
    return dot(high, table_high) + dot(low, table_high) + dot(high, table_low)


def alternating(shape):
    lane = lax.broadcasted_iota(jnp.int32, shape, 1)
    return jnp.where(lane % 2 == 0, 1.0, -1.0).astype(F32)


def vmem():
    return pl.BlockSpec(memory_space=pltpu.VMEM)


def smem():
    return pl.BlockSpec(memory_space=pltpu.SMEM)


MOVES = ((0, 0), (2, 1), (2, 0), (1, 1), (3, 1), (1, 0), (3, 0), (0, 1))


def target_shard(shard, move):
    return lax.rem(shard // 2 + move[0], 4) * 2 + lax.rem(shard % 2 + move[1], 2)


def source_shard(shard, move):
    return lax.rem(shard // 2 + 4 - move[0], 4) * 2 + lax.rem(shard % 2 + move[1], 2)


def rim_kernel(prev_first, now_first, psi_first, prev_last, now_last, psi_last, initial, last):
    rows = prev_last.shape[1]
    initial[:, 0:1] = psi_first[:, 0:1]
    initial[:, 1:2] = now_first[:, 0:1]
    initial[:, 2:4] = prev_first[:, 0:2]
    last[:, 0:1] = psi_last[:, rows - 1 :]
    last[:, 1:2] = now_last[:, rows - 1 :]
    last[:, 2:4] = prev_last[:, rows - 2 :]


def rims(q_prev, q_now, psi_now):
    layers, rows, cols = q_prev.shape
    first = pl.BlockSpec((layers, 8, cols), lambda i: (0, 0, 0))
    final = pl.BlockSpec((layers, 8, cols), lambda i: (0, rows // 8 - 1, 0))
    rim = jax.ShapeDtypeStruct((layers, 4, cols), F32)
    whole = pl.BlockSpec(rim.shape, lambda i: (0, 0, 0))
    return pl.pallas_call(
        rim_kernel,
        grid=(1,),
        in_specs=[first, first, first, final, final, final],
        out_specs=[whole, whole],
        out_shape=[rim, rim],
        compiler_params=params(62),
        name="rims",
    )(q_prev, q_now, psi_now, q_prev, q_now, psi_now)


def shift_columns(source, to_east, to_west):
    count, rows, width = source.shape
    lane = lax.broadcasted_iota(jnp.int32, (rows, width), 1)
    east, west = {count: 0.0}, {-1: 0.0}

    def store(c):
        to_east[c] = jnp.where(lane == width - 1, east[c + 1], east[c])
        to_west[c] = jnp.where(lane == 0, west[c - 1], west[c])

    for c in range(count + LAG):
        if c < count:
            value = source[c]
            east[c] = pltpu.roll(value, width - 1, 1)
            west[c] = pltpu.roll(value, 1, 1)
        if c >= LAG:
            store(c - LAG)


def advance(fields, segments, rows, store):
    p, z, ze, zw, q, qe, qw = fields
    count, _, width = p.shape
    lane = lax.broadcasted_iota(jnp.int32, (rows, width), 1)
    third = -2.0 * TIME_STEP / 12.0
    drag = -2.0 * TIME_STEP * VISCOSITY
    middle = {}
    east = {(n, count): 0.0 for n in range(len(segments))}
    west = {(n, -1): 0.0 for n in range(len(segments))}

    def tendency(n, c):
        start, wall = segments[n]

        def here(ext, row=0):
            return ext[c, start + row : start + row + rows, :]

        pn, pc, ps = here(p, -1), here(p), here(p, 1)
        zn, zc, zs = here(z, -1), here(z), here(z, 1)
        zne, zce, zse = here(ze, -1), here(ze), here(ze, 1)
        znw, zcw, zsw = here(zw, -1), here(zw), here(zw, 1)
        qc = here(q)
        near = here(q, -1) + here(q, 1)
        far = here(q, -2) + here(q, 2)
        down = zs - zn
        beside = 2.0 * near - 8.0 * qc
        from_east = pc * ((zsw - znw) + down) + ps * (zsw - zc) + pn * (zc - znw)
        from_west = ps * (zc - zse) + pn * (zne - zc) - pc * ((zse - zne) + down)
        from_east = third * from_east + drag * (beside + here(qe))
        from_west = third * from_west + drag * (beside + here(qw))
        east[n, c] = pltpu.roll(from_east, width - 1, 1)
        west[n, c] = pltpu.roll(from_west, 1, 1)
        across = zce - zcw
        own = pn * (across + (zne - znw)) - ps * (across + (zse - zsw))
        bulk = far - 8.0 * near + 20.0 * qc
        if wall is not None:
            bulk = bulk - wall * qc
        if c == 0:
            bulk = bulk - jnp.where(lane == 0, qc, 0.0)
        if c == count - 1:
            bulk = bulk - jnp.where(lane == width - 1, qc, 0.0)
        middle[n, c] = qc + third * own + drag * bulk

    def finish(n, c):
        value = middle[n, c] + jnp.where(lane == width - 1, east[n, c + 1], east[n, c])
        store(n, c, value + jnp.where(lane == 0, west[n, c - 1], west[n, c]))

    for c in range(count + LAG):
        for n in range(len(segments)):
            if c < count:
                tendency(n, c)
            if c >= LAG:
                finish(n, c - LAG)


def fold_columns(count, rows, read, write):
    lane = lax.broadcasted_iota(jnp.int32, (rows, LANES), 1)
    order = LANES - 1 - lane
    sign = alternating((rows, LANES))
    pairs = {}
    for c in range(count // 2 + LAG):
        if c < count // 2:
            pairs[c] = read(c), jnp.take_along_axis(read(count - 1 - c), order, axis=1)
        if c >= LAG:
            lower, upper = pairs[c - LAG]
            write(c - LAG, (lower + upper) * sign, lower - upper)


def inner_kernel(prev, now, psi, table_high_in, table_low_in, q_out, high, low, rim, near, table_high, table_low, *scratch):
    fields, q_held, p, z, ze, zw, q, qe, qw, sems, q_sems, table_sems = scratch
    layers, rows, cols = prev.shape
    inner = rows - 16
    layer = pl.program_id(0)

    def load(index, which):
        source = (psi, now, prev)[which]
        slot = index % 2
        return pltpu.make_async_copy(source.at[index], fields.at[slot, which], sems.at[slot, which])

    def save(index):
        return pltpu.make_async_copy(
            q_held.at[index, pl.ds(8, inner)], q_out.at[index, pl.ds(8, inner)], q_sems.at[index]
        )

    tables = [
        pltpu.make_async_copy(table_high_in, table_high, table_sems.at[0]),
        pltpu.make_async_copy(table_low_in, table_low, table_sems.at[1]),
    ]

    @pl.when(layer == 0)
    def _():
        for index in range(2):
            for which in range(3):
                load(index, which).start()

    for which in range(3):
        load(layer, which).wait()
    for which, ext in enumerate((p, z, q)):
        for c in range(ext.shape[0]):
            ext[c, 8 : 8 + rows, :] = fields[layer % 2, which, :, LANES * c : LANES * (c + 1)]
        near[which, layer, 0:4] = fields[layer % 2, which, 0:4]
        near[which, layer, 4:8] = fields[layer % 2, which, rows - 4 :]

    @pl.when(layer + 2 < layers)
    def _():
        for which in range(3):
            load(layer + 2, which).start()

    @pl.when(layer == layers - 2)
    def _():
        for table in tables:
            table.start()

    shift_columns(z, ze, zw)
    shift_columns(q, qe, qw)

    def store(n, c, value):
        q_held[layer, :, LANES * c : LANES * (c + 1)] = value

    advance((p, z, ze, zw, q, qe, qw), [(8, None)], rows, store)
    save(layer).start()
    rim[layer, 0:8] = q_held[layer, 0:8]
    rim[layer, 8:16] = q_held[layer, rows - 8 :]

    def read(c):
        return q_held[layer, 8 : 8 + inner, LANES * c : LANES * (c + 1)]

    def write(c, *folds):
        for parity, value in enumerate(folds):
            line = pl.ds(pl.multiple_of((parity * layers + layer) * inner, inner), inner)
            column = slice(LANES * c, LANES * (c + 1))
            high[line, column], low[line, column] = split(value)

    fold_columns(cols // LANES, inner, read, write)

    @pl.when(layer == layers - 1)
    def _():
        for index in range(layers):
            save(index).wait()
        for table in tables:
            table.wait()


def inner_step(q_prev, q_now, psi_now, table_high, table_low):
    layers, rows, cols = q_prev.shape
    depth = cols // 2
    hbm = pl.BlockSpec(memory_space=pltpu.HBM)
    lines = jax.ShapeDtypeStruct((2 * layers * (rows - 16), depth), BF16)
    table = jax.ShapeDtypeStruct((depth, depth), BF16)
    return pl.pallas_call(
        inner_kernel,
        grid=(layers,),
        in_specs=[hbm] * 5,
        out_specs=[hbm] + [vmem()] * 6,
        out_shape=[
            jax.ShapeDtypeStruct(q_prev.shape, F32),
            lines,
            lines,
            jax.ShapeDtypeStruct((layers, 16, cols), F32),
            jax.ShapeDtypeStruct((3, layers, 8, cols), F32),
            table,
            table,
        ],
        scratch_shapes=[pltpu.VMEM((2, 3, rows, cols), F32), pltpu.VMEM((layers, rows, cols), F32)]
        + [pltpu.VMEM((cols // LANES, rows + 16, LANES), F32)] * 7
        + [
            pltpu.SemaphoreType.DMA((2, 3)),
            pltpu.SemaphoreType.DMA((layers,)),
            pltpu.SemaphoreType.DMA((2,)),
        ],
        compiler_params=params(INNER_LIMIT),
        cost_estimate=pl.CostEstimate(flops=60 * layers * rows * cols, bytes_accessed=12 << 20, transcendentals=0),
        name="inner_step",
    )(q_prev, q_now, psi_now, table_high, table_low)


def outer_kernel(blocks, place, shard, top, bottom, high_in, low_in, rim, near, table_high, table_low, q_in, q_out, *refs):
    leaving, scratch = refs[: len(MOVES)], refs[len(MOVES) :]
    q_rim, p, z, ze, zw, q, qe, qw, high, low, held, q_sems = scratch
    layers, _, cols = rim.shape
    shards, lines, width = held.shape
    width //= 2
    rows = lines // layers
    inner = rows - 16

    for n in range(layers):
        first, last = 8 + 32 * n, 24 + 32 * n
        for which, (ext, row, size) in enumerate(((p, 0, 1), (z, 1, 1), (q, 2, 2))):
            for c in range(cols // LANES):
                column = slice(LANES * c, LANES * (c + 1))
                ext[c, first - size : first, :] = top[n, row : row + size, column]
                ext[c, first : first + 4, :] = near[which, n, 0:4, column]
                ext[c, last + 4 : last + 8, :] = near[which, n, 4:8, column]
                ext[c, last + 8 : last + 8 + size, :] = bottom[n, row : row + size, column]
    shift_columns(z, ze, zw)
    shift_columns(q, qe, qw)
    row = lax.broadcasted_iota(jnp.int32, (8, LANES), 0)
    wall_above = jnp.where(row == jnp.where(place[0] == 0, 0, -1), 1.0, 0.0).astype(F32)
    wall_below = jnp.where(row == jnp.where(place[0] == blocks - 1, 7, -1), 1.0, 0.0).astype(F32)
    segments = []
    for n in range(layers):
        segments += [(8 + 32 * n, wall_above), (24 + 32 * n, wall_below)]

    def store(n, c, value):
        at, column = slice(8 * (n % 2), 8 * (n % 2) + 8), slice(LANES * c, LANES * (c + 1))
        fresh = row >= 6 if n % 2 else row < 2
        q_rim[n // 2, at, column] = jnp.where(fresh, value, rim[n // 2, at, column])

    advance((p, z, ze, zw, q, qe, qw), segments, 8, store)

    def save(n, edge):
        source = q_rim.at[n, pl.ds(8 * edge, 8)]
        return pltpu.make_async_copy(source, q_out.at[n, pl.ds((rows - 8) * edge, 8)], q_sems.at[n, edge])

    for n in range(layers):
        for edge in range(2):
            save(n, edge).start()

    for block in range(2 * layers):
        line = slice(block * rows, block * rows + inner)
        high[line, :] = high_in[block * inner : (block + 1) * inner, :]
        low[line, :] = low_in[block * inner : (block + 1) * inner, :]
    for n in range(layers):

        def read(c):
            return q_rim[n, :, LANES * c : LANES * (c + 1)]

        def write(c, *folds):
            for parity, value in enumerate(folds):
                start = (parity * layers + n) * rows + inner
                column = slice(LANES * c, LANES * (c + 1))
                high[start : start + 16, column], low[start : start + 16, column] = split(value)

        fold_columns(cols // LANES, 16, read, write)

    def columns(step, carry):
        span = pl.ds(pl.multiple_of(step * 2 * width, 2 * width), 2 * width)
        value = three_dots(high[...], low[...], table_high[:, span], table_low[:, span])
        for part in range(2):
            column = slice(part * width, (part + 1) * width)
            for parity in range(2):
                lane = slice(parity * width, (parity + 1) * width)
                for n in range(layers):
                    start, to = (parity * layers + n) * rows, n * rows
                    held[2 * step + part, to + 8 : to + 8 + inner, lane] = value[start : start + inner, column]
                    held[2 * step + part, to : to + 8, lane] = value[start + inner : start + inner + 8, column]
                    held[2 * step + part, to + rows - 8 : to + rows, lane] = value[start + rows - 8 : start + rows, column]
        return carry

    lax.fori_loop(0, shards // 2, columns, 0)
    for move, piece in zip(MOVES, leaving):
        piece[...] = held[target_shard(shard[0], move)]
    for n in range(layers):
        for edge in range(2):
            save(n, edge).wait()


def outer_step(place, shard, top, bottom, high, low, rim, near, table_high, table_low, q_next, shards, blocks):
    layers, rows, cols = q_next.shape
    depth = cols // 2
    lines = layers * rows
    width = depth // shards
    hbm = pl.BlockSpec(memory_space=pltpu.HBM)
    return pl.pallas_call(
        functools.partial(outer_kernel, blocks),
        in_specs=[smem()] * 2 + [vmem()] * 8 + [hbm],
        out_specs=[hbm] + [vmem()] * len(MOVES),
        out_shape=[jax.ShapeDtypeStruct(q_next.shape, F32)]
        + [jax.ShapeDtypeStruct((lines, 2 * width), F32)] * len(MOVES),
        input_output_aliases={10: 0},
        scratch_shapes=[pltpu.VMEM((layers, 16, cols), F32)]
        + [pltpu.VMEM((cols // LANES, 32 * layers + 8, LANES), F32)] * 7
        + [pltpu.VMEM((2 * lines, depth), BF16)] * 2
        + [
            pltpu.VMEM((shards, lines, 2 * width), F32),
            pltpu.SemaphoreType.DMA((layers, 2)),
        ],
        compiler_params=params(OUTER_LIMIT),
        cost_estimate=pl.CostEstimate(flops=12 * lines * depth * depth, bytes_accessed=4 << 20, transcendentals=0),
        name="outer_step",
    )(place, shard, top, bottom, high, low, rim, near, table_high, table_low, q_next)


def choose(which, piece):
    total = 0
    for number, move in enumerate(MOVES):
        total = total + jnp.where(piece == number, move[which], 0)
    return total


def prepare_kernel(shard, eigen, stretch, to_modes, to_layers, theta, ratio, scale, in_high, in_low, out_high, out_low):
    modes, width = theta.shape
    wave = eigen[pl.ds(shard[0], 1), :]
    for mode in range(modes):
        theta[mode : mode + 1, :] = wave + stretch[mode]
    shift = theta[...]
    half = 0.5 * jnp.sqrt(shift)
    angle = 2.0 * jnp.log1p(half + half * half / (1.0 + jnp.sqrt(1.0 + half * half)))
    theta[...] = angle
    ratio[...] = jnp.exp(-angle)
    scale[...] = (-2.0 / (width * eigen.shape[0] + 1)) / jnp.sqrt(shift * (4.0 + shift))

    size = 8 * modes
    line = lax.broadcasted_iota(jnp.int32, (size, modes), 0)
    index = lax.broadcasted_iota(jnp.int32, (size, modes), 1)

    piece = line // (size // len(MOVES))
    share = modes // len(MOVES)

    def layer_of(around, across):
        other = lax.rem(shard[0] // 2 + around, 4) * 2 + lax.rem(shard[0] % 2 + across, 2)
        return (other * share + (line // 8) % share == index).astype(F32)

    arriving = layer_of(4 - choose(0, piece), choose(1, piece))
    leaving = layer_of(choose(0, piece), choose(1, piece))
    by_mode = (line % modes == index).astype(F32)
    down = lax.broadcasted_iota(jnp.int32, (size, size), 0)
    along = lax.broadcasted_iota(jnp.int32, (size, size), 1)

    def exact(left, right, sides):
        return lax.dot_general(
            left, right, ((sides, ((), ()))), precision=lax.Precision.HIGHEST, preferred_element_type=F32
        )

    spread = exact(exact(by_mode, to_modes[...], ((1,), (0,))), arriving, ((1,), (1,)))
    in_high[...], in_low[...] = split(jnp.where(down // modes == along % 8, spread, 0.0))
    spread = exact(exact(leaving, to_layers[...], ((1,), (0,))), by_mode, ((1,), (1,)))
    out_high[...], out_low[...] = split(jnp.where(down % 8 == along // modes, spread, 0.0))


def prepare(shard, eigen, stretch, to_modes, to_layers):
    modes, width = stretch.shape[0], eigen.shape[1]
    field = jax.ShapeDtypeStruct((modes, width), F32)
    mix = jax.ShapeDtypeStruct((8 * modes, 8 * modes), BF16)
    return pl.pallas_call(
        prepare_kernel,
        in_specs=[smem(), vmem(), smem(), vmem(), vmem()],
        out_specs=[vmem()] * 7,
        out_shape=[field, field, field, mix, mix, mix, mix],
        compiler_params=params(8),
        name="prepare",
    )(shard, eigen, stretch, to_modes, to_layers)


def project_kernel(mix_high, mix_low, ratio, *refs):
    pieces, (modal, ends) = refs[:-2], refs[-2:]
    rows, layers, width = modal.shape
    share = layers // len(pieces)
    decay = ratio[...]

    def tile(t, sums):
        last, first, scale = sums
        at = pl.ds(pl.multiple_of(8 * t, 8), 8)
        lines = [piece[:, at, :].reshape(8 * share, width) for piece in pieces]
        high, low = split(jnp.concatenate(lines, axis=0))
        mixed = dot(mix_high[...], high) + dot(mix_low[...], high) + dot(mix_high[...], low)
        block = mixed.reshape(8, layers, width)
        modal[at] = block
        for row in range(8):
            last = decay * last + block[row]
            first = first + scale * block[row]
            scale = scale * decay
        return last, first, scale

    zeros = jnp.zeros((layers, width), F32)
    last, first, _ = lax.fori_loop(0, rows // 8, tile, (zeros, zeros, zeros + 1.0), unroll=2)
    ends[0] = last
    ends[1] = first


def project(pieces, mix_high, mix_low, ratio):
    share, rows, width = pieces[0].shape
    layers = share * len(pieces)
    return pl.pallas_call(
        project_kernel,
        in_specs=[vmem()] * (3 + len(pieces)),
        out_specs=[vmem()] * 2,
        out_shape=[
            jax.ShapeDtypeStruct((rows, layers, width), F32),
            jax.ShapeDtypeStruct((2, layers, width), F32),
        ],
        compiler_params=params(8),
        name="project",
    )(mix_high, mix_low, ratio, *pieces)


RADICES = (2, 4, 4)


def exchange(total, level, blocks):
    radix, group = RADICES[level], math.prod(RADICES[:level])
    parts = []
    for shift in range(1, radix):
        pairs = []
        for target in range(blocks):
            spot = (target // group) % radix
            pairs.append((target + ((spot + shift) % radix - spot) * group, target))
        parts.append(lax.ppermute(total, "row", pairs))
    return parts


def decayed(unit, count):
    return jnp.exp(-unit * count.astype(F32))


def join(unit, me, parts, level):
    radix, group = RADICES[level], math.prod(RADICES[:level])
    place = (me // group) % radix
    last = jnp.zeros_like(unit)
    first = jnp.zeros_like(unit)
    for shift, part in enumerate(parts):
        spot = (place + shift) % radix
        last = last + decayed(unit, group * (radix - 1 - spot)) * part[0]
        first = first + decayed(unit, group * spot) * part[1]
    return last, first


def join_kernel(level, rows, place, theta, *refs):
    parts, result = refs[:-1], refs[-1]
    last, first = join(rows * theta[...], place[0], parts, level)
    result[0] = last
    result[1] = first


def join_level(level, rows, place, theta, parts):
    return pl.pallas_call(
        functools.partial(join_kernel, level, rows),
        in_specs=[smem(), vmem()] + [vmem()] * len(parts),
        out_specs=vmem(),
        out_shape=jax.ShapeDtypeStruct(parts[0].shape, F32),
        compiler_params=params(8),
        name="join",
    )(place, theta, *parts)


def entering(theta, rows, me, blocks, levels):
    unit = rows * theta
    above = jnp.zeros_like(theta)
    below = jnp.zeros_like(theta)
    for level, parts in enumerate(levels):
        radix, group = RADICES[level], math.prod(RADICES[:level])
        spot_here, inside = (me // group) % radix, me % group
        for shift in range(1, radix):
            spot = (spot_here + shift) % radix
            over = jnp.maximum(group * (spot_here - 1 - spot), 0) + inside
            under = jnp.maximum(group * (spot - spot_here - 1), 0) + group - 1 - inside
            above = above + jnp.where(spot < spot_here, decayed(unit, over), 0.0) * parts[shift][0]
            below = below + jnp.where(spot > spot_here, decayed(unit, under), 0.0) * parts[shift][1]
    last, first = join(unit, me, levels[-1], len(levels) - 1)
    span = jnp.exp(-theta * (rows * blocks + 1))
    wall = jnp.exp(-theta) / (1.0 - span * span)
    above = above + decayed(unit, me) * wall * (span * last - first)
    below = below + decayed(unit, blocks - 1 - me) * wall * (span * first - last)
    return above, below


def solve_kernel(blocks, place, theta, modal, ratio, scale, mix_high, mix_low, *refs):
    count = sum(RADICES)
    parts, results, down = refs[:count], refs[count:-1], refs[-1]
    rows, layers, width = modal.shape
    share = layers // len(results)
    decay, factor = ratio[...], scale[...]
    levels, at = [], 0
    for radix in RADICES:
        levels.append(parts[at : at + radix])
        at += radix
    above, below = entering(theta[...], rows, place[0], blocks, levels)

    def forth(row, value):
        value = decay * value + modal[row]
        down[row] = value
        return value

    lax.fori_loop(0, rows, forth, above, unroll=8)

    def tile(step, beyond):
        base = pl.multiple_of(rows - 8 * (step + 1), 8)
        solved = [None] * 8
        for row in range(7, -1, -1):
            value = decay * beyond
            beyond = modal[base + row] + value
            solved[row] = factor * (down[base + row] + value)
        high, low = split(jnp.stack(solved).reshape(8 * layers, width))
        mixed = dot(mix_high[...], high) + dot(mix_low[...], high) + dot(mix_high[...], low)
        for number, result in enumerate(results):
            piece = mixed[8 * share * number : 8 * share * (number + 1)]
            result[:, pl.ds(base, 8), :] = piece.reshape(share, 8, width)
        return beyond

    lax.fori_loop(0, rows // 8, tile, below, unroll=2)


def solve(place, theta, modal, ratio, scale, mix_high, mix_low, parts, blocks):
    rows, layers, width = modal.shape
    return pl.pallas_call(
        functools.partial(solve_kernel, blocks),
        in_specs=[smem()] + [vmem()] * (6 + len(parts)),
        out_specs=[vmem()] * len(MOVES),
        out_shape=[jax.ShapeDtypeStruct((layers // len(MOVES), rows, width), F32)] * len(MOVES),
        scratch_shapes=[pltpu.VMEM((rows, layers, width), F32)],
        compiler_params=params(12),
        name="solve",
    )(place, theta, modal, ratio, scale, mix_high, mix_low, *parts)


def gather_pieces(shard, numbers, pieces, table_high, table_low, high, low, rows_high, rows_low):
    lines, width = pieces[0].shape
    width //= 2
    for slot, (number, piece) in enumerate(zip(numbers, pieces)):
        column = slice(slot * width, (slot + 1) * width)
        for parity in range(2):
            line = slice(parity * lines, (parity + 1) * lines)
            high[line, column], low[line, column] = split(piece[:, parity * width : (parity + 1) * width])
        at = pl.ds(pl.multiple_of(source_shard(shard, MOVES[number]) * width, width), width)
        rows_high[column, :] = table_high[at, :]
        rows_low[column, :] = table_low[at, :]


def inverse_part_kernel(numbers, shard, table_high, table_low, *refs):
    pieces, (result, *scratch) = refs[: len(numbers)], refs[len(numbers) :]
    gather_pieces(shard[0], numbers, pieces, table_high, table_low, *scratch)
    high, low, rows_high, rows_low = scratch
    step = 256
    for start in range(0, result.shape[1], step):
        span = slice(start, start + step)
        result[:, span] = three_dots(high[...], low[...], rows_high[:, span], rows_low[:, span])


def inverse_rest_kernel(numbers, shard, table_high, table_low, partial, *refs):
    pieces, (result, high, low, rows_high, rows_low, held, sems) = refs[: len(numbers)], refs[len(numbers) :]
    gather_pieces(shard[0], numbers, pieces, table_high, table_low, high, low, rows_high, rows_low)
    count, lines, step = held.shape
    order = LANES - 1 - lax.broadcasted_iota(jnp.int32, (lines, LANES), 1)
    sign = alternating((1, step))

    def copy(block):
        return pltpu.make_async_copy(held.at[block], result.at[:, pl.ds(block * step, step)], sems.at[block])

    for index in range(count // 2):
        span = slice(index * step, (index + 1) * step)
        value = partial[:, span] + three_dots(high[...], low[...], rows_high[:, span], rows_low[:, span])
        odd, even = value[:lines] * sign, value[lines:]
        held[index] = odd + even
        copy(index).start()
        mirror = odd - even
        for part in range(step // LANES):
            block = mirror[:, step - LANES * (part + 1) : step - LANES * part]
            held[count - 1 - index, :, LANES * part : LANES * (part + 1)] = jnp.take_along_axis(block, order, axis=1)
        copy(count - 1 - index).start()
    for block in range(count):
        copy(block).wait()


def inverse(shard, pieces, table_high, table_low, first):
    lines, width = pieces[0].shape
    depth = len(pieces) * width // 2
    step = 256
    count = 2 * depth // step

    def scratch(taken):
        columns = taken * width // 2
        return [pltpu.VMEM((2 * lines, columns), BF16)] * 2 + [pltpu.VMEM((columns, depth), BF16)] * 2

    numbers = tuple(range(first))
    partial = pl.pallas_call(
        functools.partial(inverse_part_kernel, numbers),
        in_specs=[smem()] + [vmem()] * (2 + first),
        out_specs=vmem(),
        out_shape=jax.ShapeDtypeStruct((2 * lines, depth), F32),
        scratch_shapes=scratch(first),
        compiler_params=params(10),
        cost_estimate=pl.CostEstimate(flops=6 * lines * depth * depth, bytes_accessed=2 << 20, transcendentals=0),
        name="inverse_part",
    )(shard, table_high, table_low, *pieces[:first])
    numbers = tuple(range(first, len(pieces)))
    return pl.pallas_call(
        functools.partial(inverse_rest_kernel, numbers),
        in_specs=[smem()] + [vmem()] * (3 + len(numbers)),
        out_specs=pl.BlockSpec(memory_space=pltpu.HBM),
        out_shape=jax.ShapeDtypeStruct((lines, 2 * depth), F32),
        scratch_shapes=scratch(len(numbers))
        + [pltpu.VMEM((count, lines, step), F32), pltpu.SemaphoreType.DMA((count,))],
        compiler_params=params(14),
        name="inverse_rest",
    )(shard, table_high, table_low, partial, *pieces[first:])


def move_pieces(leaving):
    shards = len(MOVES)
    arrived = leaving[:1]
    for (around, across), piece in zip(MOVES[1:], leaving[1:]):
        pairs = [(i, ((i // 2 + around) % 4) * 2 + (i % 2 + across) % 2) for i in range(shards)]
        arrived.append(lax.ppermute(piece, "layer", pairs))
    return arrived


def on_device(q_prev, q_now, psi_now, layers_to_modes, modes_to_layers, stretch):
    layer_count, row_count, col_count = q_prev.shape
    blocks = lax.axis_size("row")
    shards = lax.axis_size("layer")
    me = lax.axis_index("row")
    table_high, table_low = (jnp.asarray(value) for value in half_table(col_count))
    eigen = jnp.asarray(column_eigen(col_count, shards))
    place = me.astype(jnp.int32).reshape(1)
    shard = lax.axis_index("layer").astype(jnp.int32).reshape(1)

    initial, last = rims(q_prev, q_now, psi_now)
    pairs = [(i, i + 1) for i in range(blocks - 1)]
    top = lax.ppermute(last, "row", pairs)
    bottom = lax.ppermute(initial, "row", [(j, i) for i, j in pairs])
    theta, ratio, scale, *mixes = prepare(shard, eigen, stretch, layers_to_modes, modes_to_layers)
    q_next, *folded, table_high, table_low = inner_step(q_prev, q_now, psi_now, table_high, table_low)
    q_next, *leaving = outer_step(
        place, shard, top, bottom, *folded, table_high, table_low, q_next, shards, blocks
    )
    arrived = move_pieces(leaving)
    arrived = [piece.reshape(layer_count, row_count, -1) for piece in arrived]
    modal, total = project(arrived, mixes[0], mixes[1], ratio)
    parts = []
    for level in range(len(RADICES)):
        group = [total] + exchange(total, level, blocks)
        parts.extend(group)
        if level + 1 < len(RADICES):
            total = join_level(level, row_count, place, theta, group)
    leaving = solve(place, theta, modal, ratio, scale, mixes[2], mixes[3], parts, blocks)
    leaving = [piece.reshape(layer_count * row_count, -1) for piece in leaving]
    pieces = move_pieces(leaving)
    psi_next = inverse(shard, pieces, table_high, table_low, 4)
    return (q_next, psi_next.reshape(q_prev.shape))


def solution(mesh):
    return jax.shard_map(
        on_device,
        mesh=mesh,
        in_specs=(
            P("layer", "row", None),
            P("layer", "row", None),
            P("layer", "row", None),
            P(),
            P(),
            P(),
        ),
        out_specs=(P("layer", "row", None), P("layer", "row", None)),
        check_vma=False,
    )
```

```python
import functools
import math

import jax
import jax.numpy as jnp
import ml_dtypes
import numpy as np
from jax import lax
from jax.experimental import pallas as pl
from jax.experimental.pallas import tpu as pltpu
from jax.sharding import PartitionSpec as P

TIME_STEP = 0.1
VISCOSITY = 0.02
F32 = jnp.float32
BF16 = jnp.bfloat16
LANES = 128
LAG = 2
INNER_LIMIT = 46
OUTER_LIMIT = 24


def params(megabytes):
    return pltpu.CompilerParams(vmem_limit_bytes=megabytes << 20)


def half_table(length):
    positions = np.arange(1, length // 2 + 1, dtype=np.int64)
    product = (2 * positions[:, None] * positions[None, :]) % (2 * (length + 1))
    table = np.sin(product.astype(np.float64) * (math.pi / (length + 1)))
    high = table.astype(np.float32).astype(ml_dtypes.bfloat16)
    low = (table - high.astype(np.float64)).astype(np.float32).astype(ml_dtypes.bfloat16)
    return high, low


def column_eigen(length, shards):
    positions = np.arange(1, length // 2 + 1, dtype=np.float64)
    waves = np.stack([length + 1 - 2 * positions, 2 * positions])
    eigen = 4.0 * np.sin(waves * (math.pi / (2 * (length + 1)))) ** 2
    eigen = eigen.astype(np.float32).reshape(2, shards, -1)
    return np.concatenate([eigen[0], eigen[1]], axis=1)


def split(value):
    high = value.astype(BF16)
    low = (value - high.astype(F32)).astype(BF16)
    return high, low


def dot(left, right):
    return jnp.dot(left, right, preferred_element_type=F32)


def three_dots(high, low, table_high, table_low):
    return dot(high, table_high) + dot(low, table_high) + dot(high, table_low)


def alternating(shape):
    lane = lax.broadcasted_iota(jnp.int32, shape, 1)
    return jnp.where(lane % 2 == 0, 1.0, -1.0).astype(F32)


def vmem():
    return pl.BlockSpec(memory_space=pltpu.VMEM)


def smem():
    return pl.BlockSpec(memory_space=pltpu.SMEM)


MOVES = ((0, 0), (2, 1), (0, 1), (2, 0), (1, 1), (3, 1), (1, 0), (3, 0))


def target_shard(shard, move):
    return lax.rem(shard // 2 + move[0], 4) * 2 + lax.rem(shard % 2 + move[1], 2)


def source_shard(shard, move):
    return lax.rem(shard // 2 + 4 - move[0], 4) * 2 + lax.rem(shard % 2 + move[1], 2)


def rim_kernel(prev_first, now_first, psi_first, prev_last, now_last, psi_last, initial, last):
    rows = prev_last.shape[1]
    initial[:, 0:1] = psi_first[:, 0:1]
    initial[:, 1:2] = now_first[:, 0:1]
    initial[:, 2:4] = prev_first[:, 0:2]
    last[:, 0:1] = psi_last[:, rows - 1 :]
    last[:, 1:2] = now_last[:, rows - 1 :]
    last[:, 2:4] = prev_last[:, rows - 2 :]


def rims(q_prev, q_now, psi_now):
    layers, rows, cols = q_prev.shape
    first = pl.BlockSpec((layers, 8, cols), lambda i: (0, 0, 0))
    final = pl.BlockSpec((layers, 8, cols), lambda i: (0, rows // 8 - 1, 0))
    rim = jax.ShapeDtypeStruct((layers, 4, cols), F32)
    whole = pl.BlockSpec(rim.shape, lambda i: (0, 0, 0))
    return pl.pallas_call(
        rim_kernel,
        grid=(1,),
        in_specs=[first, first, first, final, final, final],
        out_specs=[whole, whole],
        out_shape=[rim, rim],
        compiler_params=params(62),
        name="rims",
    )(q_prev, q_now, psi_now, q_prev, q_now, psi_now)


def shift_columns(source, to_east, to_west):
    count, rows, width = source.shape
    lane = lax.broadcasted_iota(jnp.int32, (rows, width), 1)
    east, west = {count: 0.0}, {-1: 0.0}

    def store(c):
        to_east[c] = jnp.where(lane == width - 1, east[c + 1], east[c])
        to_west[c] = jnp.where(lane == 0, west[c - 1], west[c])

    for c in range(count + LAG):
        if c < count:
            value = source[c]
            east[c] = pltpu.roll(value, width - 1, 1)
            west[c] = pltpu.roll(value, 1, 1)
        if c >= LAG:
            store(c - LAG)


def advance(fields, segments, rows, store):
    p, z, ze, zw, q, qe, qw = fields
    count, _, width = p.shape
    lane = lax.broadcasted_iota(jnp.int32, (rows, width), 1)
    third = -2.0 * TIME_STEP / 12.0
    drag = -2.0 * TIME_STEP * VISCOSITY
    middle = {}
    east = {(n, count): 0.0 for n in range(len(segments))}
    west = {(n, -1): 0.0 for n in range(len(segments))}

    def tendency(n, c):
        start, wall = segments[n]

        def here(ext, row=0):
            return ext[c, start + row : start + row + rows, :]

        pn, pc, ps = here(p, -1), here(p), here(p, 1)
        zn, zc, zs = here(z, -1), here(z), here(z, 1)
        zne, zce, zse = here(ze, -1), here(ze), here(ze, 1)
        znw, zcw, zsw = here(zw, -1), here(zw), here(zw, 1)
        qc = here(q)
        near = here(q, -1) + here(q, 1)
        far = here(q, -2) + here(q, 2)
        down = zs - zn
        beside = 2.0 * near - 8.0 * qc
        from_east = pc * ((zsw - znw) + down) + ps * (zsw - zc) + pn * (zc - znw)
        from_west = ps * (zc - zse) + pn * (zne - zc) - pc * ((zse - zne) + down)
        from_east = third * from_east + drag * (beside + here(qe))
        from_west = third * from_west + drag * (beside + here(qw))
        east[n, c] = pltpu.roll(from_east, width - 1, 1)
        west[n, c] = pltpu.roll(from_west, 1, 1)
        across = zce - zcw
        own = pn * (across + (zne - znw)) - ps * (across + (zse - zsw))
        bulk = far - 8.0 * near + 20.0 * qc
        if wall is not None:
            bulk = bulk - wall * qc
        if c == 0:
            bulk = bulk - jnp.where(lane == 0, qc, 0.0)
        if c == count - 1:
            bulk = bulk - jnp.where(lane == width - 1, qc, 0.0)
        middle[n, c] = qc + third * own + drag * bulk

    def finish(n, c):
        value = middle[n, c] + jnp.where(lane == width - 1, east[n, c + 1], east[n, c])
        store(n, c, value + jnp.where(lane == 0, west[n, c - 1], west[n, c]))

    for c in range(count + LAG):
        for n in range(len(segments)):
            if c < count:
                tendency(n, c)
            if c >= LAG:
                finish(n, c - LAG)


def fold_columns(count, rows, read, write):
    lane = lax.broadcasted_iota(jnp.int32, (rows, LANES), 1)
    order = LANES - 1 - lane
    sign = alternating((rows, LANES))
    pairs = {}
    for c in range(count // 2 + LAG):
        if c < count // 2:
            pairs[c] = read(c), jnp.take_along_axis(read(count - 1 - c), order, axis=1)
        if c >= LAG:
            lower, upper = pairs[c - LAG]
            write(c - LAG, (lower + upper) * sign, lower - upper)


def inner_kernel(prev, now, psi, table_high_in, table_low_in, q_out, high, low, rim, near, table_high, table_low, *scratch):
    fields, q_held, p, z, ze, zw, q, qe, qw, sems, q_sems, table_sems = scratch
    layers, rows, cols = prev.shape
    inner = rows - 16
    layer = pl.program_id(0)

    def load(index, which):
        source = (psi, now, prev)[which]
        slot = index % 2
        return pltpu.make_async_copy(source.at[index], fields.at[slot, which], sems.at[slot, which])

    def save(index):
        return pltpu.make_async_copy(
            q_held.at[index, pl.ds(8, inner)], q_out.at[index, pl.ds(8, inner)], q_sems.at[index]
        )

    tables = [
        pltpu.make_async_copy(table_high_in, table_high, table_sems.at[0]),
        pltpu.make_async_copy(table_low_in, table_low, table_sems.at[1]),
    ]

    @pl.when(layer == 0)
    def _():
        for index in range(2):
            for which in range(3):
                load(index, which).start()

    for which in range(3):
        load(layer, which).wait()
    for which, ext in enumerate((p, z, q)):
        for c in range(ext.shape[0]):
            ext[c, 8 : 8 + rows, :] = fields[layer % 2, which, :, LANES * c : LANES * (c + 1)]
        near[which, layer, 0:4] = fields[layer % 2, which, 0:4]
        near[which, layer, 4:8] = fields[layer % 2, which, rows - 4 :]

    @pl.when(layer + 2 < layers)
    def _():
        for which in range(3):
            load(layer + 2, which).start()

    @pl.when(layer == layers - 2)
    def _():
        for table in tables:
            table.start()

    shift_columns(z, ze, zw)
    shift_columns(q, qe, qw)

    def store(n, c, value):
        q_held[layer, :, LANES * c : LANES * (c + 1)] = value

    advance((p, z, ze, zw, q, qe, qw), [(8, None)], rows, store)
    save(layer).start()
    rim[layer, 0:8] = q_held[layer, 0:8]
    rim[layer, 8:16] = q_held[layer, rows - 8 :]

    def read(c):
        return q_held[layer, 8 : 8 + inner, LANES * c : LANES * (c + 1)]

    def write(c, *folds):
        for parity, value in enumerate(folds):
            line = pl.ds(pl.multiple_of((parity * layers + layer) * inner, inner), inner)
            column = slice(LANES * c, LANES * (c + 1))
            high[line, column], low[line, column] = split(value)

    fold_columns(cols // LANES, inner, read, write)

    @pl.when(layer == layers - 1)
    def _():
        for index in range(layers):
            save(index).wait()
        for table in tables:
            table.wait()


def inner_step(q_prev, q_now, psi_now, table_high, table_low):
    layers, rows, cols = q_prev.shape
    depth = cols // 2
    hbm = pl.BlockSpec(memory_space=pltpu.HBM)
    lines = jax.ShapeDtypeStruct((2 * layers * (rows - 16), depth), BF16)
    table = jax.ShapeDtypeStruct((depth, depth), BF16)
    return pl.pallas_call(
        inner_kernel,
        grid=(layers,),
        in_specs=[hbm] * 5,
        out_specs=[hbm] + [vmem()] * 6,
        out_shape=[
            jax.ShapeDtypeStruct(q_prev.shape, F32),
            lines,
            lines,
            jax.ShapeDtypeStruct((layers, 16, cols), F32),
            jax.ShapeDtypeStruct((3, layers, 8, cols), F32),
            table,
            table,
        ],
        scratch_shapes=[pltpu.VMEM((2, 3, rows, cols), F32), pltpu.VMEM((layers, rows, cols), F32)]
        + [pltpu.VMEM((cols // LANES, rows + 16, LANES), F32)] * 7
        + [
            pltpu.SemaphoreType.DMA((2, 3)),
            pltpu.SemaphoreType.DMA((layers,)),
            pltpu.SemaphoreType.DMA((2,)),
        ],
        compiler_params=params(INNER_LIMIT),
        cost_estimate=pl.CostEstimate(flops=60 * layers * rows * cols, bytes_accessed=12 << 20, transcendentals=0),
        name="inner_step",
    )(q_prev, q_now, psi_now, table_high, table_low)


def outer_kernel(blocks, place, shard, top, bottom, high_in, low_in, rim, near, table_high, table_low, q_in, q_out, *refs):
    leaving, scratch = refs[: len(MOVES)], refs[len(MOVES) :]
    q_rim, p, z, ze, zw, q, qe, qw, high, low, held, q_sems = scratch
    layers, _, cols = rim.shape
    shards, lines, width = held.shape
    width //= 2
    rows = lines // layers
    inner = rows - 16

    for n in range(layers):
        first, last = 8 + 32 * n, 24 + 32 * n
        for which, (ext, row, size) in enumerate(((p, 0, 1), (z, 1, 1), (q, 2, 2))):
            for c in range(cols // LANES):
                column = slice(LANES * c, LANES * (c + 1))
                ext[c, first - size : first, :] = top[n, row : row + size, column]
                ext[c, first : first + 4, :] = near[which, n, 0:4, column]
                ext[c, last + 4 : last + 8, :] = near[which, n, 4:8, column]
                ext[c, last + 8 : last + 8 + size, :] = bottom[n, row : row + size, column]
    shift_columns(z, ze, zw)
    shift_columns(q, qe, qw)
    row = lax.broadcasted_iota(jnp.int32, (8, LANES), 0)
    wall_above = jnp.where(row == jnp.where(place[0] == 0, 0, -1), 1.0, 0.0).astype(F32)
    wall_below = jnp.where(row == jnp.where(place[0] == blocks - 1, 7, -1), 1.0, 0.0).astype(F32)
    segments = []
    for n in range(layers):
        segments += [(8 + 32 * n, wall_above), (24 + 32 * n, wall_below)]

    def store(n, c, value):
        at, column = slice(8 * (n % 2), 8 * (n % 2) + 8), slice(LANES * c, LANES * (c + 1))
        fresh = row >= 6 if n % 2 else row < 2
        q_rim[n // 2, at, column] = jnp.where(fresh, value, rim[n // 2, at, column])

    advance((p, z, ze, zw, q, qe, qw), segments, 8, store)

    def save(n, edge):
        source = q_rim.at[n, pl.ds(8 * edge, 8)]
        return pltpu.make_async_copy(source, q_out.at[n, pl.ds((rows - 8) * edge, 8)], q_sems.at[n, edge])

    for n in range(layers):
        for edge in range(2):
            save(n, edge).start()

    for block in range(2 * layers):
        line = slice(block * rows, block * rows + inner)
        high[line, :] = high_in[block * inner : (block + 1) * inner, :]
        low[line, :] = low_in[block * inner : (block + 1) * inner, :]
    for n in range(layers):

        def read(c):
            return q_rim[n, :, LANES * c : LANES * (c + 1)]

        def write(c, *folds):
            for parity, value in enumerate(folds):
                start = (parity * layers + n) * rows + inner
                column = slice(LANES * c, LANES * (c + 1))
                high[start : start + 16, column], low[start : start + 16, column] = split(value)

        fold_columns(cols // LANES, 16, read, write)

    def columns(step, carry):
        span = pl.ds(pl.multiple_of(step * 2 * width, 2 * width), 2 * width)
        value = three_dots(high[...], low[...], table_high[:, span], table_low[:, span])
        for part in range(2):
            column = slice(part * width, (part + 1) * width)
            for parity in range(2):
                lane = slice(parity * width, (parity + 1) * width)
                for n in range(layers):
                    start, to = (parity * layers + n) * rows, n * rows
                    held[2 * step + part, to + 8 : to + 8 + inner, lane] = value[start : start + inner, column]
                    held[2 * step + part, to : to + 8, lane] = value[start + inner : start + inner + 8, column]
                    held[2 * step + part, to + rows - 8 : to + rows, lane] = value[start + rows - 8 : start + rows, column]
        return carry

    lax.fori_loop(0, shards // 2, columns, 0)
    for move, piece in zip(MOVES, leaving):
        piece[...] = held[target_shard(shard[0], move)]
    for n in range(layers):
        for edge in range(2):
            save(n, edge).wait()


def outer_step(place, shard, top, bottom, high, low, rim, near, table_high, table_low, q_next, shards, blocks):
    layers, rows, cols = q_next.shape
    depth = cols // 2
    lines = layers * rows
    width = depth // shards
    hbm = pl.BlockSpec(memory_space=pltpu.HBM)
    return pl.pallas_call(
        functools.partial(outer_kernel, blocks),
        in_specs=[smem()] * 2 + [vmem()] * 8 + [hbm],
        out_specs=[hbm] + [vmem()] * len(MOVES),
        out_shape=[jax.ShapeDtypeStruct(q_next.shape, F32)]
        + [jax.ShapeDtypeStruct((lines, 2 * width), F32)] * len(MOVES),
        input_output_aliases={10: 0},
        scratch_shapes=[pltpu.VMEM((layers, 16, cols), F32)]
        + [pltpu.VMEM((cols // LANES, 32 * layers + 8, LANES), F32)] * 7
        + [pltpu.VMEM((2 * lines, depth), BF16)] * 2
        + [
            pltpu.VMEM((shards, lines, 2 * width), F32),
            pltpu.SemaphoreType.DMA((layers, 2)),
        ],
        compiler_params=params(OUTER_LIMIT),
        cost_estimate=pl.CostEstimate(flops=12 * lines * depth * depth, bytes_accessed=4 << 20, transcendentals=0),
        name="outer_step",
    )(place, shard, top, bottom, high, low, rim, near, table_high, table_low, q_next)


def choose(which, piece):
    total = 0
    for number, move in enumerate(MOVES):
        total = total + jnp.where(piece == number, move[which], 0)
    return total


def prepare_kernel(shard, eigen, stretch, to_modes, to_layers, theta, ratio, scale, in_high, in_low, out_high, out_low):
    modes, width = theta.shape
    wave = eigen[pl.ds(shard[0], 1), :]
    for mode in range(modes):
        theta[mode : mode + 1, :] = wave + stretch[mode]
    shift = theta[...]
    half = 0.5 * jnp.sqrt(shift)
    angle = 2.0 * jnp.log1p(half + half * half / (1.0 + jnp.sqrt(1.0 + half * half)))
    theta[...] = angle
    ratio[...] = jnp.exp(-angle)
    scale[...] = (-2.0 / (width * eigen.shape[0] + 1)) / jnp.sqrt(shift * (4.0 + shift))

    size = 8 * modes
    line = lax.broadcasted_iota(jnp.int32, (size, modes), 0)
    index = lax.broadcasted_iota(jnp.int32, (size, modes), 1)

    piece = line // (size // len(MOVES))
    share = modes // len(MOVES)

    def layer_of(around, across):
        other = lax.rem(shard[0] // 2 + around, 4) * 2 + lax.rem(shard[0] % 2 + across, 2)
        return (other * share + (line // 8) % share == index).astype(F32)

    arriving = layer_of(4 - choose(0, piece), choose(1, piece))
    leaving = layer_of(choose(0, piece), choose(1, piece))
    by_mode = (line % modes == index).astype(F32)
    down = lax.broadcasted_iota(jnp.int32, (size, size), 0)
    along = lax.broadcasted_iota(jnp.int32, (size, size), 1)

    def exact(left, right, sides):
        return lax.dot_general(
            left, right, ((sides, ((), ()))), precision=lax.Precision.HIGHEST, preferred_element_type=F32
        )

    spread = exact(exact(by_mode, to_modes[...], ((1,), (0,))), arriving, ((1,), (1,)))
    in_high[...], in_low[...] = split(jnp.where(down // modes == along % 8, spread, 0.0))
    spread = exact(exact(leaving, to_layers[...], ((1,), (0,))), by_mode, ((1,), (1,)))
    out_high[...], out_low[...] = split(jnp.where(down % 8 == along // modes, spread, 0.0))


def prepare(shard, eigen, stretch, to_modes, to_layers):
    modes, width = stretch.shape[0], eigen.shape[1]
    field = jax.ShapeDtypeStruct((modes, width), F32)
    mix = jax.ShapeDtypeStruct((8 * modes, 8 * modes), BF16)
    return pl.pallas_call(
        prepare_kernel,
        in_specs=[smem(), vmem(), smem(), vmem(), vmem()],
        out_specs=[vmem()] * 7,
        out_shape=[field, field, field, mix, mix, mix, mix],
        compiler_params=params(8),
        name="prepare",
    )(shard, eigen, stretch, to_modes, to_layers)


def project_kernel(mix_high, mix_low, ratio, *refs):
    pieces, (modal, ends) = refs[:-2], refs[-2:]
    rows, layers, width = modal.shape
    share = layers // len(pieces)
    decay = ratio[...]

    def tile(t, sums):
        last, first, scale = sums
        at = pl.ds(pl.multiple_of(8 * t, 8), 8)
        lines = [piece[:, at, :].reshape(8 * share, width) for piece in pieces]
        high, low = split(jnp.concatenate(lines, axis=0))
        mixed = dot(mix_high[...], high) + dot(mix_low[...], high) + dot(mix_high[...], low)
        block = mixed.reshape(8, layers, width)
        modal[at] = block
        for row in range(8):
            last = decay * last + block[row]
            first = first + scale * block[row]
            scale = scale * decay
        return last, first, scale

    zeros = jnp.zeros((layers, width), F32)
    last, first, _ = lax.fori_loop(0, rows // 8, tile, (zeros, zeros, zeros + 1.0), unroll=2)
    ends[0] = last
    ends[1] = first


def project(pieces, mix_high, mix_low, ratio):
    share, rows, width = pieces[0].shape
    layers = share * len(pieces)
    return pl.pallas_call(
        project_kernel,
        in_specs=[vmem()] * (3 + len(pieces)),
        out_specs=[vmem()] * 2,
        out_shape=[
            jax.ShapeDtypeStruct((rows, layers, width), F32),
            jax.ShapeDtypeStruct((2, layers, width), F32),
        ],
        compiler_params=params(8),
        name="project",
    )(mix_high, mix_low, ratio, *pieces)


RADICES = (2, 4, 4)


def exchange(total, level, blocks):
    radix, group = RADICES[level], math.prod(RADICES[:level])
    parts = {}
    for shift in sorted(range(1, radix), key=lambda shift: min(shift, radix - shift)):
        pairs = []
        for target in range(blocks):
            spot = (target // group) % radix
            pairs.append((target + ((spot + shift) % radix - spot) * group, target))
        parts[shift] = lax.ppermute(total, "row", pairs)
    return [parts[shift] for shift in range(1, radix)]


def decayed(unit, count):
    return jnp.exp(-unit * count.astype(F32))


def join(unit, me, parts, level):
    radix, group = RADICES[level], math.prod(RADICES[:level])
    place = (me // group) % radix
    last = jnp.zeros_like(unit)
    first = jnp.zeros_like(unit)
    for shift, part in enumerate(parts):
        spot = (place + shift) % radix
        last = last + decayed(unit, group * (radix - 1 - spot)) * part[0]
        first = first + decayed(unit, group * spot) * part[1]
    return last, first


def join_kernel(level, rows, place, theta, *refs):
    parts, result = refs[:-1], refs[-1]
    last, first = join(rows * theta[...], place[0], parts, level)
    result[0] = last
    result[1] = first


def join_level(level, rows, place, theta, parts):
    return pl.pallas_call(
        functools.partial(join_kernel, level, rows),
        in_specs=[smem(), vmem()] + [vmem()] * len(parts),
        out_specs=vmem(),
        out_shape=jax.ShapeDtypeStruct(parts[0].shape, F32),
        compiler_params=params(8),
        name="join",
    )(place, theta, *parts)


def entering(theta, rows, me, blocks, levels):
    unit = rows * theta
    above = jnp.zeros_like(theta)
    below = jnp.zeros_like(theta)
    for level, parts in enumerate(levels):
        radix, group = RADICES[level], math.prod(RADICES[:level])
        spot_here, inside = (me // group) % radix, me % group
        for shift in range(1, radix):
            spot = (spot_here + shift) % radix
            over = jnp.maximum(group * (spot_here - 1 - spot), 0) + inside
            under = jnp.maximum(group * (spot - spot_here - 1), 0) + group - 1 - inside
            above = above + jnp.where(spot < spot_here, decayed(unit, over), 0.0) * parts[shift][0]
            below = below + jnp.where(spot > spot_here, decayed(unit, under), 0.0) * parts[shift][1]
    last, first = join(unit, me, levels[-1], len(levels) - 1)
    span = jnp.exp(-theta * (rows * blocks + 1))
    wall = jnp.exp(-theta) / (1.0 - span * span)
    above = above + decayed(unit, me) * wall * (span * last - first)
    below = below + decayed(unit, blocks - 1 - me) * wall * (span * first - last)
    return above, below


def solve_kernel(blocks, place, theta, modal, ratio, scale, mix_high, mix_low, *refs):
    count = sum(RADICES)
    parts, results, down = refs[:count], refs[count:-1], refs[-1]
    rows, layers, width = modal.shape
    share = layers // len(results)
    decay, factor = ratio[...], scale[...]
    levels, at = [], 0
    for radix in RADICES:
        levels.append(parts[at : at + radix])
        at += radix
    above, below = entering(theta[...], rows, place[0], blocks, levels)

    def forth(row, value):
        value = decay * value + modal[row]
        down[row] = value
        return value

    lax.fori_loop(0, rows, forth, above, unroll=8)

    def tile(step, beyond):
        base = pl.multiple_of(rows - 8 * (step + 1), 8)
        solved = [None] * 8
        for row in range(7, -1, -1):
            value = decay * beyond
            beyond = modal[base + row] + value
            solved[row] = factor * (down[base + row] + value)
        high, low = split(jnp.stack(solved).reshape(8 * layers, width))
        mixed = dot(mix_high[...], high) + dot(mix_low[...], high) + dot(mix_high[...], low)
        for number, result in enumerate(results):
            piece = mixed[8 * share * number : 8 * share * (number + 1)]
            result[:, pl.ds(base, 8), :] = piece.reshape(share, 8, width)
        return beyond

    lax.fori_loop(0, rows // 8, tile, below, unroll=2)


def solve(place, theta, modal, ratio, scale, mix_high, mix_low, parts, blocks):
    rows, layers, width = modal.shape
    return pl.pallas_call(
        functools.partial(solve_kernel, blocks),
        in_specs=[smem()] + [vmem()] * (6 + len(parts)),
        out_specs=[vmem()] * len(MOVES),
        out_shape=[jax.ShapeDtypeStruct((layers // len(MOVES), rows, width), F32)] * len(MOVES),
        scratch_shapes=[pltpu.VMEM((rows, layers, width), F32)],
        compiler_params=params(12),
        name="solve",
    )(place, theta, modal, ratio, scale, mix_high, mix_low, *parts)


def gather_pieces(shard, numbers, pieces, table_high, table_low, high, low, rows_high, rows_low):
    lines, width = pieces[0].shape
    width //= 2
    for slot, (number, piece) in enumerate(zip(numbers, pieces)):
        column = slice(slot * width, (slot + 1) * width)
        for parity in range(2):
            line = slice(parity * lines, (parity + 1) * lines)
            high[line, column], low[line, column] = split(piece[:, parity * width : (parity + 1) * width])
        at = pl.ds(pl.multiple_of(source_shard(shard, MOVES[number]) * width, width), width)
        rows_high[column, :] = table_high[at, :]
        rows_low[column, :] = table_low[at, :]


def inverse_part_kernel(numbers, shard, table_high, table_low, *refs):
    pieces, (result, *scratch) = refs[: len(numbers)], refs[len(numbers) :]
    gather_pieces(shard[0], numbers, pieces, table_high, table_low, *scratch)
    high, low, rows_high, rows_low = scratch
    step = 256
    for start in range(0, result.shape[1], step):
        span = slice(start, start + step)
        result[:, span] = three_dots(high[...], low[...], rows_high[:, span], rows_low[:, span])


def inverse_rest_kernel(numbers, shard, table_high, table_low, partial, *refs):
    pieces, (result, high, low, rows_high, rows_low, held, sems) = refs[: len(numbers)], refs[len(numbers) :]
    gather_pieces(shard[0], numbers, pieces, table_high, table_low, high, low, rows_high, rows_low)
    count, lines, step = held.shape
    order = LANES - 1 - lax.broadcasted_iota(jnp.int32, (lines, LANES), 1)
    sign = alternating((1, step))

    def copy(block):
        return pltpu.make_async_copy(held.at[block], result.at[:, pl.ds(block * step, step)], sems.at[block])

    for index in range(count // 2):
        span = slice(index * step, (index + 1) * step)
        value = partial[:, span] + three_dots(high[...], low[...], rows_high[:, span], rows_low[:, span])
        odd, even = value[:lines] * sign, value[lines:]
        held[index] = odd + even
        copy(index).start()
        mirror = odd - even
        for part in range(step // LANES):
            block = mirror[:, step - LANES * (part + 1) : step - LANES * part]
            held[count - 1 - index, :, LANES * part : LANES * (part + 1)] = jnp.take_along_axis(block, order, axis=1)
        copy(count - 1 - index).start()
    for block in range(count):
        copy(block).wait()


def inverse(shard, pieces, table_high, table_low, first):
    lines, width = pieces[0].shape
    depth = len(pieces) * width // 2
    step = 256
    count = 2 * depth // step

    def scratch(taken):
        columns = taken * width // 2
        return [pltpu.VMEM((2 * lines, columns), BF16)] * 2 + [pltpu.VMEM((columns, depth), BF16)] * 2

    numbers = tuple(range(first))
    partial = pl.pallas_call(
        functools.partial(inverse_part_kernel, numbers),
        in_specs=[smem()] + [vmem()] * (2 + first),
        out_specs=vmem(),
        out_shape=jax.ShapeDtypeStruct((2 * lines, depth), F32),
        scratch_shapes=scratch(first),
        compiler_params=params(10),
        cost_estimate=pl.CostEstimate(flops=6 * lines * depth * depth, bytes_accessed=2 << 20, transcendentals=0),
        name="inverse_part",
    )(shard, table_high, table_low, *pieces[:first])
    numbers = tuple(range(first, len(pieces)))
    return pl.pallas_call(
        functools.partial(inverse_rest_kernel, numbers),
        in_specs=[smem()] + [vmem()] * (3 + len(numbers)),
        out_specs=pl.BlockSpec(memory_space=pltpu.HBM),
        out_shape=jax.ShapeDtypeStruct((lines, 2 * depth), F32),
        scratch_shapes=scratch(len(numbers))
        + [pltpu.VMEM((count, lines, step), F32), pltpu.SemaphoreType.DMA((count,))],
        compiler_params=params(14),
        name="inverse_rest",
    )(shard, table_high, table_low, partial, *pieces[first:])


def move_pieces(leaving):
    shards = len(MOVES)
    arrived = leaving[:1]
    for (around, across), piece in zip(MOVES[1:], leaving[1:]):
        pairs = [(i, ((i // 2 + around) % 4) * 2 + (i % 2 + across) % 2) for i in range(shards)]
        arrived.append(lax.ppermute(piece, "layer", pairs))
    return arrived


def on_device(q_prev, q_now, psi_now, layers_to_modes, modes_to_layers, stretch):
    layer_count, row_count, col_count = q_prev.shape
    blocks = lax.axis_size("row")
    shards = lax.axis_size("layer")
    me = lax.axis_index("row")
    table_high, table_low = (jnp.asarray(value) for value in half_table(col_count))
    eigen = jnp.asarray(column_eigen(col_count, shards))
    place = me.astype(jnp.int32).reshape(1)
    shard = lax.axis_index("layer").astype(jnp.int32).reshape(1)

    initial, last = rims(q_prev, q_now, psi_now)
    pairs = [(i, i + 1) for i in range(blocks - 1)]
    top = lax.ppermute(last, "row", pairs)
    bottom = lax.ppermute(initial, "row", [(j, i) for i, j in pairs])
    theta, ratio, scale, *mixes = prepare(shard, eigen, stretch, layers_to_modes, modes_to_layers)
    q_next, *folded, table_high, table_low = inner_step(q_prev, q_now, psi_now, table_high, table_low)
    q_next, *leaving = outer_step(
        place, shard, top, bottom, *folded, table_high, table_low, q_next, shards, blocks
    )
    arrived = move_pieces(leaving)
    arrived = [piece.reshape(layer_count, row_count, -1) for piece in arrived]
    modal, total = project(arrived, mixes[0], mixes[1], ratio)
    parts = []
    for level in range(len(RADICES)):
        group = [total] + exchange(total, level, blocks)
        parts.extend(group)
        if level + 1 < len(RADICES):
            total = join_level(level, row_count, place, theta, group)
    leaving = solve(place, theta, modal, ratio, scale, mixes[2], mixes[3], parts, blocks)
    leaving = [piece.reshape(layer_count * row_count, -1) for piece in leaving]
    pieces = move_pieces(leaving)
    psi_next = inverse(shard, pieces, table_high, table_low, 4)
    return (q_next, psi_next.reshape(q_prev.shape))


def solution(mesh):
    return jax.shard_map(
        on_device,
        mesh=mesh,
        in_specs=(
            P("layer", "row", None),
            P("layer", "row", None),
            P("layer", "row", None),
            P(),
            P(),
            P(),
        ),
        out_specs=(P("layer", "row", None), P("layer", "row", None)),
        check_vma=False,
    )
```

```python
import functools
import math

import jax
import jax.numpy as jnp
import ml_dtypes
import numpy as np
from jax import lax
from jax.experimental import pallas as pl
from jax.experimental.pallas import tpu as pltpu
from jax.sharding import PartitionSpec as P

TIME_STEP = 0.1
VISCOSITY = 0.02
F32 = jnp.float32
BF16 = jnp.bfloat16
LANES = 128
LAG = 2
INNER_LIMIT = 46
OUTER_LIMIT = 24


def params(megabytes):
    return pltpu.CompilerParams(vmem_limit_bytes=megabytes << 20)


def half_table(length):
    positions = np.arange(1, length // 2 + 1, dtype=np.int64)
    product = (2 * positions[:, None] * positions[None, :]) % (2 * (length + 1))
    table = np.sin(product.astype(np.float64) * (math.pi / (length + 1)))
    high = table.astype(np.float32).astype(ml_dtypes.bfloat16)
    low = (table - high.astype(np.float64)).astype(np.float32).astype(ml_dtypes.bfloat16)
    return high, low


def column_eigen(length, shards):
    positions = np.arange(1, length // 2 + 1, dtype=np.float64)
    waves = np.stack([length + 1 - 2 * positions, 2 * positions])
    eigen = 4.0 * np.sin(waves * (math.pi / (2 * (length + 1)))) ** 2
    eigen = eigen.astype(np.float32).reshape(2, shards, -1)
    return np.concatenate([eigen[0], eigen[1]], axis=1)


def split(value):
    high = value.astype(BF16)
    low = (value - high.astype(F32)).astype(BF16)
    return high, low


def dot(left, right):
    return jnp.dot(left, right, preferred_element_type=F32)


def three_dots(high, low, table_high, table_low):
    return dot(high, table_high) + dot(low, table_high) + dot(high, table_low)


def alternating(shape):
    lane = lax.broadcasted_iota(jnp.int32, shape, 1)
    return jnp.where(lane % 2 == 0, 1.0, -1.0).astype(F32)


def vmem():
    return pl.BlockSpec(memory_space=pltpu.VMEM)


def smem():
    return pl.BlockSpec(memory_space=pltpu.SMEM)


MOVES = ((0, 0), (2, 1), (0, 1), (2, 0), (1, 1), (3, 1), (1, 0), (3, 0))


def target_shard(shard, move):
    return lax.rem(shard // 2 + move[0], 4) * 2 + lax.rem(shard % 2 + move[1], 2)


def source_shard(shard, move):
    return lax.rem(shard // 2 + 4 - move[0], 4) * 2 + lax.rem(shard % 2 + move[1], 2)


def rim_kernel(prev_first, now_first, psi_first, prev_last, now_last, psi_last, initial, last):
    rows = prev_last.shape[1]
    initial[:, 0:1] = psi_first[:, 0:1]
    initial[:, 1:2] = now_first[:, 0:1]
    initial[:, 2:4] = prev_first[:, 0:2]
    last[:, 0:1] = psi_last[:, rows - 1 :]
    last[:, 1:2] = now_last[:, rows - 1 :]
    last[:, 2:4] = prev_last[:, rows - 2 :]


def rims(q_prev, q_now, psi_now):
    layers, rows, cols = q_prev.shape
    first = pl.BlockSpec((layers, 8, cols), lambda i: (0, 0, 0))
    final = pl.BlockSpec((layers, 8, cols), lambda i: (0, rows // 8 - 1, 0))
    rim = jax.ShapeDtypeStruct((layers, 4, cols), F32)
    whole = pl.BlockSpec(rim.shape, lambda i: (0, 0, 0))
    return pl.pallas_call(
        rim_kernel,
        grid=(1,),
        in_specs=[first, first, first, final, final, final],
        out_specs=[whole, whole],
        out_shape=[rim, rim],
        compiler_params=params(62),
        name="rims",
    )(q_prev, q_now, psi_now, q_prev, q_now, psi_now)


def shift_columns(source, to_east, to_west):
    count, rows, width = source.shape
    lane = lax.broadcasted_iota(jnp.int32, (rows, width), 1)
    east, west = {count: 0.0}, {-1: 0.0}

    def store(c):
        to_east[c] = jnp.where(lane == width - 1, east[c + 1], east[c])
        to_west[c] = jnp.where(lane == 0, west[c - 1], west[c])

    for c in range(count + LAG):
        if c < count:
            value = source[c]
            east[c] = pltpu.roll(value, width - 1, 1)
            west[c] = pltpu.roll(value, 1, 1)
        if c >= LAG:
            store(c - LAG)


def advance(fields, segments, rows, store):
    p, z, ze, zw, q, qe, qw = fields
    count, _, width = p.shape
    lane = lax.broadcasted_iota(jnp.int32, (rows, width), 1)
    third = -2.0 * TIME_STEP / 12.0
    drag = -2.0 * TIME_STEP * VISCOSITY
    middle = {}
    east = {(n, count): 0.0 for n in range(len(segments))}
    west = {(n, -1): 0.0 for n in range(len(segments))}

    def tendency(n, c):
        start, wall = segments[n]

        def here(ext, row=0):
            return ext[c, start + row : start + row + rows, :]

        pn, pc, ps = here(p, -1), here(p), here(p, 1)
        zn, zc, zs = here(z, -1), here(z), here(z, 1)
        zne, zce, zse = here(ze, -1), here(ze), here(ze, 1)
        znw, zcw, zsw = here(zw, -1), here(zw), here(zw, 1)
        qc = here(q)
        near = here(q, -1) + here(q, 1)
        far = here(q, -2) + here(q, 2)
        down = zs - zn
        beside = 2.0 * near - 8.0 * qc
        from_east = pc * ((zsw - znw) + down) + ps * (zsw - zc) + pn * (zc - znw)
        from_west = ps * (zc - zse) + pn * (zne - zc) - pc * ((zse - zne) + down)
        from_east = third * from_east + drag * (beside + here(qe))
        from_west = third * from_west + drag * (beside + here(qw))
        east[n, c] = pltpu.roll(from_east, width - 1, 1)
        west[n, c] = pltpu.roll(from_west, 1, 1)
        across = zce - zcw
        own = pn * (across + (zne - znw)) - ps * (across + (zse - zsw))
        bulk = far - 8.0 * near + 20.0 * qc
        if wall is not None:
            bulk = bulk - wall * qc
        if c == 0:
            bulk = bulk - jnp.where(lane == 0, qc, 0.0)
        if c == count - 1:
            bulk = bulk - jnp.where(lane == width - 1, qc, 0.0)
        middle[n, c] = qc + third * own + drag * bulk

    def finish(n, c):
        value = middle[n, c] + jnp.where(lane == width - 1, east[n, c + 1], east[n, c])
        store(n, c, value + jnp.where(lane == 0, west[n, c - 1], west[n, c]))

    for c in range(count + LAG):
        for n in range(len(segments)):
            if c < count:
                tendency(n, c)
            if c >= LAG:
                finish(n, c - LAG)


def fold_columns(count, rows, read, write):
    lane = lax.broadcasted_iota(jnp.int32, (rows, LANES), 1)
    order = LANES - 1 - lane
    sign = alternating((rows, LANES))
    pairs = {}
    for c in range(count // 2 + LAG):
        if c < count // 2:
            pairs[c] = read(c), jnp.take_along_axis(read(count - 1 - c), order, axis=1)
        if c >= LAG:
            lower, upper = pairs[c - LAG]
            write(c - LAG, (lower + upper) * sign, lower - upper)


def inner_kernel(prev, now, psi, q_out, high, low, rim, near, *scratch):
    fields, q_held, p, z, ze, zw, q, qe, qw, sems, q_sems = scratch
    layers, rows, cols = prev.shape
    inner = rows - 16
    layer = pl.program_id(0)

    def load(index, which):
        source = (psi, now, prev)[which]
        slot = index % 2
        return pltpu.make_async_copy(source.at[index], fields.at[slot, which], sems.at[slot, which])

    def save(index):
        return pltpu.make_async_copy(
            q_held.at[index, pl.ds(8, inner)], q_out.at[index, pl.ds(8, inner)], q_sems.at[index]
        )

    @pl.when(layer == 0)
    def _():
        for index in range(2):
            for which in range(3):
                load(index, which).start()

    for which in range(3):
        load(layer, which).wait()
    for which, ext in enumerate((p, z, q)):
        for c in range(ext.shape[0]):
            ext[c, 8 : 8 + rows, :] = fields[layer % 2, which, :, LANES * c : LANES * (c + 1)]
        near[which, layer, 0:4] = fields[layer % 2, which, 0:4]
        near[which, layer, 4:8] = fields[layer % 2, which, rows - 4 :]

    @pl.when(layer + 2 < layers)
    def _():
        for which in range(3):
            load(layer + 2, which).start()

    shift_columns(z, ze, zw)
    shift_columns(q, qe, qw)

    def store(n, c, value):
        q_held[layer, :, LANES * c : LANES * (c + 1)] = value

    advance((p, z, ze, zw, q, qe, qw), [(8, None)], rows, store)
    save(layer).start()
    rim[layer, 0:8] = q_held[layer, 0:8]
    rim[layer, 8:16] = q_held[layer, rows - 8 :]

    def read(c):
        return q_held[layer, 8 : 8 + inner, LANES * c : LANES * (c + 1)]

    def write(c, *folds):
        for parity, value in enumerate(folds):
            line = pl.ds(pl.multiple_of((parity * layers + layer) * inner, inner), inner)
            column = slice(LANES * c, LANES * (c + 1))
            high[line, column], low[line, column] = split(value)

    fold_columns(cols // LANES, inner, read, write)

    @pl.when(layer == layers - 1)
    def _():
        for index in range(layers):
            save(index).wait()


def inner_step(q_prev, q_now, psi_now):
    layers, rows, cols = q_prev.shape
    depth = cols // 2
    hbm = pl.BlockSpec(memory_space=pltpu.HBM)
    lines = jax.ShapeDtypeStruct((2 * layers * (rows - 16), depth), BF16)
    return pl.pallas_call(
        inner_kernel,
        grid=(layers,),
        in_specs=[hbm] * 3,
        out_specs=[hbm] + [vmem()] * 4,
        out_shape=[
            jax.ShapeDtypeStruct(q_prev.shape, F32),
            lines,
            lines,
            jax.ShapeDtypeStruct((layers, 16, cols), F32),
            jax.ShapeDtypeStruct((3, layers, 8, cols), F32),
        ],
        scratch_shapes=[pltpu.VMEM((2, 3, rows, cols), F32), pltpu.VMEM((layers, rows, cols), F32)]
        + [pltpu.VMEM((cols // LANES, rows + 16, LANES), F32)] * 7
        + [
            pltpu.SemaphoreType.DMA((2, 3)),
            pltpu.SemaphoreType.DMA((layers,)),
        ],
        compiler_params=params(INNER_LIMIT),
        cost_estimate=pl.CostEstimate(flops=60 * layers * rows * cols, bytes_accessed=12 << 20, transcendentals=0),
        name="inner_step",
    )(q_prev, q_now, psi_now)


def outer_kernel(blocks, place, shard, top, bottom, high_in, low_in, rim, near, table_high_in, table_low_in, q_in, q_out, table_high, table_low, *refs):
    leaving, scratch = refs[: len(MOVES)], refs[len(MOVES) :]
    q_rim, p, z, ze, zw, q, qe, qw, high, low, held, q_sems, table_sems = scratch
    tables = [
        pltpu.make_async_copy(table_high_in, table_high, table_sems.at[0]),
        pltpu.make_async_copy(table_low_in, table_low, table_sems.at[1]),
    ]
    for table in tables:
        table.start()
    layers, _, cols = rim.shape
    shards, lines, width = held.shape
    width //= 2
    rows = lines // layers
    inner = rows - 16

    for n in range(layers):
        first, last = 8 + 32 * n, 24 + 32 * n
        for which, (ext, row, size) in enumerate(((p, 0, 1), (z, 1, 1), (q, 2, 2))):
            for c in range(cols // LANES):
                column = slice(LANES * c, LANES * (c + 1))
                ext[c, first - size : first, :] = top[n, row : row + size, column]
                ext[c, first : first + 4, :] = near[which, n, 0:4, column]
                ext[c, last + 4 : last + 8, :] = near[which, n, 4:8, column]
                ext[c, last + 8 : last + 8 + size, :] = bottom[n, row : row + size, column]
    shift_columns(z, ze, zw)
    shift_columns(q, qe, qw)
    row = lax.broadcasted_iota(jnp.int32, (8, LANES), 0)
    wall_above = jnp.where(row == jnp.where(place[0] == 0, 0, -1), 1.0, 0.0).astype(F32)
    wall_below = jnp.where(row == jnp.where(place[0] == blocks - 1, 7, -1), 1.0, 0.0).astype(F32)
    segments = []
    for n in range(layers):
        segments += [(8 + 32 * n, wall_above), (24 + 32 * n, wall_below)]

    def store(n, c, value):
        at, column = slice(8 * (n % 2), 8 * (n % 2) + 8), slice(LANES * c, LANES * (c + 1))
        fresh = row >= 6 if n % 2 else row < 2
        q_rim[n // 2, at, column] = jnp.where(fresh, value, rim[n // 2, at, column])

    advance((p, z, ze, zw, q, qe, qw), segments, 8, store)

    def save(n, edge):
        source = q_rim.at[n, pl.ds(8 * edge, 8)]
        return pltpu.make_async_copy(source, q_out.at[n, pl.ds((rows - 8) * edge, 8)], q_sems.at[n, edge])

    for n in range(layers):
        for edge in range(2):
            save(n, edge).start()

    for block in range(2 * layers):
        line = slice(block * rows, block * rows + inner)
        high[line, :] = high_in[block * inner : (block + 1) * inner, :]
        low[line, :] = low_in[block * inner : (block + 1) * inner, :]
    for n in range(layers):

        def read(c):
            return q_rim[n, :, LANES * c : LANES * (c + 1)]

        def write(c, *folds):
            for parity, value in enumerate(folds):
                start = (parity * layers + n) * rows + inner
                column = slice(LANES * c, LANES * (c + 1))
                high[start : start + 16, column], low[start : start + 16, column] = split(value)

        fold_columns(cols // LANES, 16, read, write)

    def columns(step, carry):
        span = pl.ds(pl.multiple_of(step * 2 * width, 2 * width), 2 * width)
        value = three_dots(high[...], low[...], table_high[:, span], table_low[:, span])
        for part in range(2):
            column = slice(part * width, (part + 1) * width)
            for parity in range(2):
                lane = slice(parity * width, (parity + 1) * width)
                for n in range(layers):
                    start, to = (parity * layers + n) * rows, n * rows
                    held[2 * step + part, to + 8 : to + 8 + inner, lane] = value[start : start + inner, column]
                    held[2 * step + part, to : to + 8, lane] = value[start + inner : start + inner + 8, column]
                    held[2 * step + part, to + rows - 8 : to + rows, lane] = value[start + rows - 8 : start + rows, column]
        return carry

    for table in tables:
        table.wait()
    lax.fori_loop(0, shards // 2, columns, 0)
    for move, piece in zip(MOVES, leaving):
        piece[...] = held[target_shard(shard[0], move)]
    for n in range(layers):
        for edge in range(2):
            save(n, edge).wait()


def outer_step(place, shard, top, bottom, high, low, rim, near, table_high, table_low, q_next, shards, blocks):
    layers, rows, cols = q_next.shape
    depth = cols // 2
    lines = layers * rows
    width = depth // shards
    hbm = pl.BlockSpec(memory_space=pltpu.HBM)
    return pl.pallas_call(
        functools.partial(outer_kernel, blocks),
        in_specs=[smem()] * 2 + [vmem()] * 6 + [hbm] * 3,
        out_specs=[hbm] + [vmem()] * (2 + len(MOVES)),
        out_shape=[jax.ShapeDtypeStruct(q_next.shape, F32)]
        + [jax.ShapeDtypeStruct((depth, depth), BF16)] * 2
        + [jax.ShapeDtypeStruct((lines, 2 * width), F32)] * len(MOVES),
        input_output_aliases={10: 0},
        scratch_shapes=[pltpu.VMEM((layers, 16, cols), F32)]
        + [pltpu.VMEM((cols // LANES, 32 * layers + 8, LANES), F32)] * 7
        + [pltpu.VMEM((2 * lines, depth), BF16)] * 2
        + [
            pltpu.VMEM((shards, lines, 2 * width), F32),
            pltpu.SemaphoreType.DMA((layers, 2)),
            pltpu.SemaphoreType.DMA((2,)),
        ],
        compiler_params=params(OUTER_LIMIT),
        cost_estimate=pl.CostEstimate(flops=12 * lines * depth * depth, bytes_accessed=4 << 20, transcendentals=0),
        name="outer_step",
    )(place, shard, top, bottom, high, low, rim, near, table_high, table_low, q_next)


def choose(which, piece):
    total = 0
    for number, move in enumerate(MOVES):
        total = total + jnp.where(piece == number, move[which], 0)
    return total


def prepare_kernel(shard, eigen, stretch, to_modes, to_layers, theta, ratio, scale, in_high, in_low, out_high, out_low):
    modes, width = theta.shape
    wave = eigen[pl.ds(shard[0], 1), :]
    for mode in range(modes):
        theta[mode : mode + 1, :] = wave + stretch[mode]
    shift = theta[...]
    half = 0.5 * jnp.sqrt(shift)
    angle = 2.0 * jnp.log1p(half + half * half / (1.0 + jnp.sqrt(1.0 + half * half)))
    theta[...] = angle
    ratio[...] = jnp.exp(-angle)
    scale[...] = (-2.0 / (width * eigen.shape[0] + 1)) / jnp.sqrt(shift * (4.0 + shift))

    size = 8 * modes
    line = lax.broadcasted_iota(jnp.int32, (size, modes), 0)
    index = lax.broadcasted_iota(jnp.int32, (size, modes), 1)

    piece = line // (size // len(MOVES))
    share = modes // len(MOVES)

    def layer_of(around, across):
        other = lax.rem(shard[0] // 2 + around, 4) * 2 + lax.rem(shard[0] % 2 + across, 2)
        return (other * share + (line // 8) % share == index).astype(F32)

    arriving = layer_of(4 - choose(0, piece), choose(1, piece))
    leaving = layer_of(choose(0, piece), choose(1, piece))
    by_mode = (line % modes == index).astype(F32)
    down = lax.broadcasted_iota(jnp.int32, (size, size), 0)
    along = lax.broadcasted_iota(jnp.int32, (size, size), 1)

    def exact(left, right, sides):
        return lax.dot_general(
            left, right, ((sides, ((), ()))), precision=lax.Precision.HIGHEST, preferred_element_type=F32
        )

    spread = exact(exact(by_mode, to_modes[...], ((1,), (0,))), arriving, ((1,), (1,)))
    in_high[...], in_low[...] = split(jnp.where(down // modes == along % 8, spread, 0.0))
    spread = exact(exact(leaving, to_layers[...], ((1,), (0,))), by_mode, ((1,), (1,)))
    out_high[...], out_low[...] = split(jnp.where(down % 8 == along // modes, spread, 0.0))


def prepare(shard, eigen, stretch, to_modes, to_layers):
    modes, width = stretch.shape[0], eigen.shape[1]
    field = jax.ShapeDtypeStruct((modes, width), F32)
    mix = jax.ShapeDtypeStruct((8 * modes, 8 * modes), BF16)
    return pl.pallas_call(
        prepare_kernel,
        in_specs=[smem(), vmem(), smem(), vmem(), vmem()],
        out_specs=[vmem()] * 7,
        out_shape=[field, field, field, mix, mix, mix, mix],
        compiler_params=params(8),
        name="prepare",
    )(shard, eigen, stretch, to_modes, to_layers)


def project_kernel(mix_high, mix_low, ratio, *refs):
    pieces, (modal, ends) = refs[:-2], refs[-2:]
    rows, layers, width = modal.shape
    share = layers // len(pieces)
    decay = ratio[...]

    def tile(t, sums):
        last, first, scale = sums
        at = pl.ds(pl.multiple_of(8 * t, 8), 8)
        lines = [piece[:, at, :].reshape(8 * share, width) for piece in pieces]
        high, low = split(jnp.concatenate(lines, axis=0))
        mixed = dot(mix_high[...], high) + dot(mix_low[...], high) + dot(mix_high[...], low)
        block = mixed.reshape(8, layers, width)
        modal[at] = block
        for row in range(8):
            last = decay * last + block[row]
            first = first + scale * block[row]
            scale = scale * decay
        return last, first, scale

    zeros = jnp.zeros((layers, width), F32)
    last, first, _ = lax.fori_loop(0, rows // 8, tile, (zeros, zeros, zeros + 1.0), unroll=2)
    ends[0] = last
    ends[1] = first


def project(pieces, mix_high, mix_low, ratio):
    share, rows, width = pieces[0].shape
    layers = share * len(pieces)
    return pl.pallas_call(
        project_kernel,
        in_specs=[vmem()] * (3 + len(pieces)),
        out_specs=[vmem()] * 2,
        out_shape=[
            jax.ShapeDtypeStruct((rows, layers, width), F32),
            jax.ShapeDtypeStruct((2, layers, width), F32),
        ],
        compiler_params=params(8),
        name="project",
    )(mix_high, mix_low, ratio, *pieces)


RADICES = (2, 4, 4)


def exchange(total, level, blocks):
    radix, group = RADICES[level], math.prod(RADICES[:level])
    parts = {}
    for shift in sorted(range(1, radix), key=lambda shift: min(shift, radix - shift)):
        pairs = []
        for target in range(blocks):
            spot = (target // group) % radix
            pairs.append((target + ((spot + shift) % radix - spot) * group, target))
        parts[shift] = lax.ppermute(total, "row", pairs)
    return [parts[shift] for shift in range(1, radix)]


def decayed(unit, count):
    return jnp.exp(-unit * count.astype(F32))


def join(unit, me, parts, level):
    radix, group = RADICES[level], math.prod(RADICES[:level])
    place = (me // group) % radix
    last = jnp.zeros_like(unit)
    first = jnp.zeros_like(unit)
    for shift, part in enumerate(parts):
        spot = (place + shift) % radix
        last = last + decayed(unit, group * (radix - 1 - spot)) * part[0]
        first = first + decayed(unit, group * spot) * part[1]
    return last, first


def join_kernel(level, rows, place, theta, *refs):
    parts, result = refs[:-1], refs[-1]
    last, first = join(rows * theta[...], place[0], parts, level)
    result[0] = last
    result[1] = first


def join_level(level, rows, place, theta, parts):
    return pl.pallas_call(
        functools.partial(join_kernel, level, rows),
        in_specs=[smem(), vmem()] + [vmem()] * len(parts),
        out_specs=vmem(),
        out_shape=jax.ShapeDtypeStruct(parts[0].shape, F32),
        compiler_params=params(8),
        name="join",
    )(place, theta, *parts)


def entering(theta, rows, me, blocks, levels):
    unit = rows * theta
    above = jnp.zeros_like(theta)
    below = jnp.zeros_like(theta)
    for level, parts in enumerate(levels):
        radix, group = RADICES[level], math.prod(RADICES[:level])
        spot_here, inside = (me // group) % radix, me % group
        for shift in range(1, radix):
            spot = (spot_here + shift) % radix
            over = jnp.maximum(group * (spot_here - 1 - spot), 0) + inside
            under = jnp.maximum(group * (spot - spot_here - 1), 0) + group - 1 - inside
            above = above + jnp.where(spot < spot_here, decayed(unit, over), 0.0) * parts[shift][0]
            below = below + jnp.where(spot > spot_here, decayed(unit, under), 0.0) * parts[shift][1]
    last, first = join(unit, me, levels[-1], len(levels) - 1)
    span = jnp.exp(-theta * (rows * blocks + 1))
    wall = jnp.exp(-theta) / (1.0 - span * span)
    above = above + decayed(unit, me) * wall * (span * last - first)
    below = below + decayed(unit, blocks - 1 - me) * wall * (span * first - last)
    return above, below


def solve_kernel(blocks, place, theta, modal, ratio, scale, mix_high, mix_low, *refs):
    count = sum(RADICES)
    parts, results, down = refs[:count], refs[count:-1], refs[-1]
    rows, layers, width = modal.shape
    share = layers // len(results)
    decay, factor = ratio[...], scale[...]
    levels, at = [], 0
    for radix in RADICES:
        levels.append(parts[at : at + radix])
        at += radix
    above, below = entering(theta[...], rows, place[0], blocks, levels)

    def forth(row, value):
        value = decay * value + modal[row]
        down[row] = value
        return value

    lax.fori_loop(0, rows, forth, above, unroll=8)

    def tile(step, beyond):
        base = pl.multiple_of(rows - 8 * (step + 1), 8)
        solved = [None] * 8
        for row in range(7, -1, -1):
            value = decay * beyond
            beyond = modal[base + row] + value
            solved[row] = factor * (down[base + row] + value)
        high, low = split(jnp.stack(solved).reshape(8 * layers, width))
        mixed = dot(mix_high[...], high) + dot(mix_low[...], high) + dot(mix_high[...], low)
        for number, result in enumerate(results):
            piece = mixed[8 * share * number : 8 * share * (number + 1)]
            result[:, pl.ds(base, 8), :] = piece.reshape(share, 8, width)
        return beyond

    lax.fori_loop(0, rows // 8, tile, below, unroll=2)


def solve(place, theta, modal, ratio, scale, mix_high, mix_low, parts, blocks):
    rows, layers, width = modal.shape
    return pl.pallas_call(
        functools.partial(solve_kernel, blocks),
        in_specs=[smem()] + [vmem()] * (6 + len(parts)),
        out_specs=[vmem()] * len(MOVES),
        out_shape=[jax.ShapeDtypeStruct((layers // len(MOVES), rows, width), F32)] * len(MOVES),
        scratch_shapes=[pltpu.VMEM((rows, layers, width), F32)],
        compiler_params=params(12),
        name="solve",
    )(place, theta, modal, ratio, scale, mix_high, mix_low, *parts)


def gather_pieces(shard, numbers, pieces, table_high, table_low, high, low, rows_high, rows_low):
    lines, width = pieces[0].shape
    width //= 2
    for slot, (number, piece) in enumerate(zip(numbers, pieces)):
        column = slice(slot * width, (slot + 1) * width)
        for parity in range(2):
            line = slice(parity * lines, (parity + 1) * lines)
            high[line, column], low[line, column] = split(piece[:, parity * width : (parity + 1) * width])
        at = pl.ds(pl.multiple_of(source_shard(shard, MOVES[number]) * width, width), width)
        rows_high[column, :] = table_high[at, :]
        rows_low[column, :] = table_low[at, :]


def inverse_part_kernel(numbers, shard, table_high, table_low, *refs):
    pieces, (result, *scratch) = refs[: len(numbers)], refs[len(numbers) :]
    gather_pieces(shard[0], numbers, pieces, table_high, table_low, *scratch)
    high, low, rows_high, rows_low = scratch
    step = 256
    for start in range(0, result.shape[1], step):
        span = slice(start, start + step)
        result[:, span] = three_dots(high[...], low[...], rows_high[:, span], rows_low[:, span])


def inverse_rest_kernel(numbers, shard, table_high, table_low, partial, *refs):
    pieces, (result, high, low, rows_high, rows_low, held, sems) = refs[: len(numbers)], refs[len(numbers) :]
    gather_pieces(shard[0], numbers, pieces, table_high, table_low, high, low, rows_high, rows_low)
    count, lines, step = held.shape
    order = LANES - 1 - lax.broadcasted_iota(jnp.int32, (lines, LANES), 1)
    sign = alternating((1, step))

    def copy(block):
        return pltpu.make_async_copy(held.at[block], result.at[:, pl.ds(block * step, step)], sems.at[block])

    for index in range(count // 2):
        span = slice(index * step, (index + 1) * step)
        value = partial[:, span] + three_dots(high[...], low[...], rows_high[:, span], rows_low[:, span])
        odd, even = value[:lines] * sign, value[lines:]
        held[index] = odd + even
        copy(index).start()
        mirror = odd - even
        for part in range(step // LANES):
            block = mirror[:, step - LANES * (part + 1) : step - LANES * part]
            held[count - 1 - index, :, LANES * part : LANES * (part + 1)] = jnp.take_along_axis(block, order, axis=1)
        copy(count - 1 - index).start()
    for block in range(count):
        copy(block).wait()


def inverse(shard, pieces, table_high, table_low, first):
    lines, width = pieces[0].shape
    depth = len(pieces) * width // 2
    step = 256
    count = 2 * depth // step

    def scratch(taken):
        columns = taken * width // 2
        return [pltpu.VMEM((2 * lines, columns), BF16)] * 2 + [pltpu.VMEM((columns, depth), BF16)] * 2

    numbers = tuple(range(first))
    partial = pl.pallas_call(
        functools.partial(inverse_part_kernel, numbers),
        in_specs=[smem()] + [vmem()] * (2 + first),
        out_specs=vmem(),
        out_shape=jax.ShapeDtypeStruct((2 * lines, depth), F32),
        scratch_shapes=scratch(first),
        compiler_params=params(10),
        cost_estimate=pl.CostEstimate(flops=6 * lines * depth * depth, bytes_accessed=2 << 20, transcendentals=0),
        name="inverse_part",
    )(shard, table_high, table_low, *pieces[:first])
    numbers = tuple(range(first, len(pieces)))
    return pl.pallas_call(
        functools.partial(inverse_rest_kernel, numbers),
        in_specs=[smem()] + [vmem()] * (3 + len(numbers)),
        out_specs=pl.BlockSpec(memory_space=pltpu.HBM),
        out_shape=jax.ShapeDtypeStruct((lines, 2 * depth), F32),
        scratch_shapes=scratch(len(numbers))
        + [pltpu.VMEM((count, lines, step), F32), pltpu.SemaphoreType.DMA((count,))],
        compiler_params=params(14),
        name="inverse_rest",
    )(shard, table_high, table_low, partial, *pieces[first:])


def move_pieces(leaving):
    shards = len(MOVES)
    arrived = leaving[:1]
    for (around, across), piece in zip(MOVES[1:], leaving[1:]):
        pairs = [(i, ((i // 2 + around) % 4) * 2 + (i % 2 + across) % 2) for i in range(shards)]
        arrived.append(lax.ppermute(piece, "layer", pairs))
    return arrived


def on_device(q_prev, q_now, psi_now, layers_to_modes, modes_to_layers, stretch):
    layer_count, row_count, col_count = q_prev.shape
    blocks = lax.axis_size("row")
    shards = lax.axis_size("layer")
    me = lax.axis_index("row")
    table_high, table_low = (jnp.asarray(value) for value in half_table(col_count))
    eigen = jnp.asarray(column_eigen(col_count, shards))
    place = me.astype(jnp.int32).reshape(1)
    shard = lax.axis_index("layer").astype(jnp.int32).reshape(1)

    initial, last = rims(q_prev, q_now, psi_now)
    pairs = [(i, i + 1) for i in range(blocks - 1)]
    top = lax.ppermute(last, "row", pairs)
    bottom = lax.ppermute(initial, "row", [(j, i) for i, j in pairs])
    theta, ratio, scale, *mixes = prepare(shard, eigen, stretch, layers_to_modes, modes_to_layers)
    q_next, *folded = inner_step(q_prev, q_now, psi_now)
    q_next, table_high, table_low, *leaving = outer_step(
        place, shard, top, bottom, *folded, table_high, table_low, q_next, shards, blocks
    )
    arrived = move_pieces(leaving)
    arrived = [piece.reshape(layer_count, row_count, -1) for piece in arrived]
    modal, total = project(arrived, mixes[0], mixes[1], ratio)
    parts = []
    for level in range(len(RADICES)):
        group = [total] + exchange(total, level, blocks)
        parts.extend(group)
        if level + 1 < len(RADICES):
            total = join_level(level, row_count, place, theta, group)
    leaving = solve(place, theta, modal, ratio, scale, mixes[2], mixes[3], parts, blocks)
    leaving = [piece.reshape(layer_count * row_count, -1) for piece in leaving]
    pieces = move_pieces(leaving)
    psi_next = inverse(shard, pieces, table_high, table_low, 4)
    return (q_next, psi_next.reshape(q_prev.shape))


def solution(mesh):
    return jax.shard_map(
        on_device,
        mesh=mesh,
        in_specs=(
            P("layer", "row", None),
            P("layer", "row", None),
            P("layer", "row", None),
            P(),
            P(),
            P(),
        ),
        out_specs=(P("layer", "row", None), P("layer", "row", None)),
        check_vma=False,
    )
```
